32 devices in a mesh: groups: 2 (over x), ex: 16 (over z, y, core).
Axes of the slice: x: 2, y: 2, z: 4, core: 2. Of those that a mesh axis runs over, the one named last changes fastest.
Arguments:
- stored_projection_inputs: bfloat16 [2, 64, 128, 8192], P(None, ('groups', 'ex')), parts along dimension 1, may hold values from -8 to 8
- key_output_gradients: bfloat16 [2, 64, 128, 1024], P(None, ('groups', 'ex')), parts along dimension 1, may hold values from -0.078125 to 0.078125
- value_output_gradients: bfloat16 [2, 64, 128, 1024], P(None, ('groups', 'ex')), parts along dimension 1, may hold values from -0.078125 to 0.078125
- key_down_factor: bfloat16 [2, 16, 8192], replicated, may hold values from -0.0625 to 0.0625
- key_up_factor: bfloat16 [2, 1024, 16], replicated, may hold values from -0.1875 to 0.1875
- value_down_factor: bfloat16 [2, 16, 8192], replicated, may hold values from -0.0625 to 0.0625
- value_up_factor: bfloat16 [2, 1024, 16], replicated, may hold values from -0.1875 to 0.1875
- validation: bfloat16 [2, 4, 294912], P(None, 'groups', 'ex'), parts along dimension 1, may hold values from -6 to 6
- lengths: int32 [64], P(('groups', 'ex')), parts along dimension 0, may hold values from 112 to 128, as said below
Outputs:
- scores: float32 [64, 2], P(('groups', 'ex')), parts along dimension 0
The draws below stay inside these ranges and needn't reach their ends.
There are 2 independent parts, one for each index of `groups`. The reference program is written for one: setup_inputs(seed, part) draws one part's arguments, and reference() takes and returns one part's arrays. A program takes and returns all parts, laid end to end along the dimension named above; an argument that names none is the same for every part. Nothing has to cross between parts.
Inputs may be any that keep to these rules, and one draw needn't show every extreme that they name: `lengths`: some example of every group has all 128 tokens.
All inputs are finite; a program needn't handle non-finite values.
Results may differ from the reference program's by a relative error of at most 0.0035.
The reference program's roundings to bfloat16 on the way count: a program that leaves them out, or rounds other values in their place, can miss the bound.
Values may be sent and summed in bfloat16 or wider, within the bound.
No kernel may reach another device: no remote copies, remote signals or barrier semaphores. Data moves between devices by JAX's collectives and lax.ppermute only.
A program may use at most 128 MiB of HBM per device.

```python
import math
import jax
import jax.numpy as jnp
from jax import lax

MODEL_DIMENSION = 8192
PROJECTION_WIDTH = 1024
ADAPTER_RANK = 16
LAYER_COUNT = 2
VALS = 2
SEQ = 128
EXAMPLES = 32


def example_scales(ramp):
    position = jnp.arange(EXAMPLES, dtype=jnp.float32) / max(EXAMPLES - 1, 1)
    return ramp ** position


def token_profile():
    tail_start = SEQ - SEQ // 8
    return jnp.where(jnp.arange(SEQ) < tail_start, 1.0, 0.4).astype(jnp.float32)


def scaled_field(shared, noise, common, ramp):
    values = jnp.clip((common * shared + noise) / math.sqrt(common * common + 1.0), -8.0, 8.0)
    sigma = 2.0 / math.sqrt(2.0 * ADAPTER_RANK * (MODEL_DIMENSION + PROJECTION_WIDTH) * SEQ)
    scales = example_scales(ramp)
    profile = token_profile()
    return (values * scales[None, :, None, None] * profile[None, None, :, None] * sigma).astype(jnp.bfloat16)


def outlier_marks(mark_key):
    count = min(16, MODEL_DIMENSION // 8)
    first, second = jax.random.split(mark_key)
    halves = jax.random.permutation(first, MODEL_DIMENSION // 2)[:count].astype(jnp.int32)
    flip = jax.random.randint(second, (), 0, 2, jnp.int32)
    parity = ((jnp.arange(count, dtype=jnp.int32) < 3 * count // 4).astype(jnp.int32) + flip) % 2
    channels = 2 * halves + parity
    return jnp.zeros((MODEL_DIMENSION,), jnp.float32).at[channels].set(1.0)


def draw_stored_projection_inputs(key, part):
    key = jax.random.fold_in(key, 11)
    first, second = jax.random.split(key)
    mark_key = jax.random.fold_in(key, 21)
    shape = (LAYER_COUNT, EXAMPLES, SEQ, MODEL_DIMENSION)
    common = 10.0
    noise = jax.random.normal(second, shape, jnp.float32)
    shared = jax.random.normal(first, (LAYER_COUNT, 1, SEQ, MODEL_DIMENSION), jnp.float32)
    values = (common * shared + noise) / math.sqrt(common * common + 1.0)
    marks = outlier_marks(mark_key)
    values = values * (1.0 + 5.0 * marks)[None, None, None, :]
    return jnp.clip(values, -8.0, 8.0).astype(jnp.bfloat16)


def draw_key_output_gradients(key, part):
    key = jax.random.fold_in(key, 12)
    first, second = jax.random.split(key)
    shape = (LAYER_COUNT, EXAMPLES, SEQ, PROJECTION_WIDTH)
    common = 10.0
    ramp = 3.0
    noise = jax.random.normal(second, shape, jnp.float32)
    shared = jax.random.normal(first, (LAYER_COUNT, 1, SEQ, PROJECTION_WIDTH), jnp.float32)
    return scaled_field(shared, noise, common, ramp)


def draw_value_output_gradients(key, part):
    key = jax.random.fold_in(key, 13)
    first, second = jax.random.split(key)
    shape = (LAYER_COUNT, EXAMPLES, SEQ, PROJECTION_WIDTH)
    common = 10.0
    ramp = 3.0
    noise = jax.random.normal(second, shape, jnp.float32)
    shared = jax.random.normal(first, (LAYER_COUNT, 1, SEQ, PROJECTION_WIDTH), jnp.float32)
    return scaled_field(shared, noise, common, ramp)


def draw_lengths(key, part):
    key = jax.random.fold_in(key, 14)
    first, second = jax.random.split(key)
    counts = jax.random.randint(first, (EXAMPLES,), SEQ - SEQ // 8, SEQ + 1, jnp.int32)
    chosen = jax.random.randint(second, (), 0, EXAMPLES, jnp.int32)
    return jnp.where(jnp.arange(EXAMPLES, dtype=jnp.int32) == chosen, SEQ, counts).astype(jnp.int32)


def shard_levels(key, shape, cuts, low, top_value):
    loudness, own = 1.0, jax.random.fold_in(key, 6)
    for axis_at, shards_of in cuts:
        heights = jnp.exp(jax.random.uniform(jax.random.fold_in(own, axis_at), (shards_of,), jnp.float32, low / len(cuts), top_value / len(cuts)))
        loudness = loudness * jnp.repeat(heights, shape[axis_at] // shards_of).reshape([-1 if axis == axis_at else 1 for axis in range(len(shape))])
    return loudness


def gaussian(stream_key, dims, spread, limit, cuts=(), kind=jnp.bfloat16):
    gain = shard_levels(stream_key, dims, cuts, -0.22, 0.18) if cuts else 1.0
    entries = jax.random.normal(stream_key, dims, jnp.float32) * spread * gain
    return jnp.minimum(jnp.maximum(entries, -limit), limit).astype(kind)


def setup_inputs(seed: int = 0, part: int = 0) -> dict:
    splits = jax.random.split(jax.random.key(seed), 10)
    own_keys = jax.random.split(jax.random.fold_in(splits[9], part), 10)
    return {
        "stored_projection_inputs": draw_stored_projection_inputs(jax.random.fold_in(jax.random.fold_in(splits[9], part), 71), part),
        "key_output_gradients": draw_key_output_gradients(jax.random.fold_in(jax.random.fold_in(splits[9], part), 71), part),
        "value_output_gradients": draw_value_output_gradients(jax.random.fold_in(jax.random.fold_in(splits[9], part), 71), part),
        "key_down_factor": gaussian(splits[3], (LAYER_COUNT, ADAPTER_RANK, MODEL_DIMENSION), MODEL_DIMENSION ** -0.5, 0.0625),
        "key_up_factor": gaussian(splits[4], (LAYER_COUNT, PROJECTION_WIDTH, ADAPTER_RANK), PROJECTION_WIDTH ** -0.5, 0.1875),
        "value_down_factor": gaussian(splits[5], (LAYER_COUNT, ADAPTER_RANK, MODEL_DIMENSION), MODEL_DIMENSION ** -0.5, 0.0625),
        "value_up_factor": gaussian(splits[6], (LAYER_COUNT, PROJECTION_WIDTH, ADAPTER_RANK), PROJECTION_WIDTH ** -0.5, 0.1875),
        "validation": gaussian(own_keys[7], (LAYER_COUNT, VALS, 2 * ADAPTER_RANK * (MODEL_DIMENSION + PROJECTION_WIDTH)), 1.0, 6.0, ((2, 16),)),
        "lengths": draw_lengths(jax.random.fold_in(jax.random.fold_in(splits[9], part), 71), part),
    }


def single_training_example(inputs, grad_key, grad_value, a_key, b_key, a_value, b_value, length):
    token_mask = (jnp.arange(SEQ) < length).astype(jnp.float32)[:, None]
    z_key = (jnp.dot(inputs, a_key.T, preferred_element_type=jnp.float32) * token_mask).astype(jnp.bfloat16)
    z_value = (jnp.dot(inputs, a_value.T, preferred_element_type=jnp.float32) * token_mask).astype(jnp.bfloat16)
    y_key = (jnp.dot(grad_key, b_key, preferred_element_type=jnp.float32) * token_mask).astype(jnp.bfloat16)
    y_value = (jnp.dot(grad_value, b_value, preferred_element_type=jnp.float32) * token_mask).astype(jnp.bfloat16)
    pieces = [
        jnp.dot(y_key.T, inputs, preferred_element_type=jnp.float32),
        jnp.dot(z_key.T, grad_key, preferred_element_type=jnp.float32),
        jnp.dot(y_value.T, inputs, preferred_element_type=jnp.float32),
        jnp.dot(z_value.T, grad_value, preferred_element_type=jnp.float32),
    ]
    return jnp.concatenate(pieces, axis=1).reshape(-1)


def reference(stored_projection_inputs, key_output_gradients, value_output_gradients, key_down_factor, key_up_factor, value_down_factor, value_up_factor, validation, lengths):
    highest = lax.Precision.HIGHEST
    scores = jnp.zeros((EXAMPLES, VALS), jnp.float32)
    for layer_position_index in range(LAYER_COUNT):
        def per_item(example_item):
            return single_training_example(example_item[0], example_item[1], example_item[2], key_down_factor[layer_position_index], key_up_factor[layer_position_index],
                               value_down_factor[layer_position_index], value_up_factor[layer_position_index], example_item[3])

        gradients = lax.map(per_item, (stored_projection_inputs[layer_position_index], key_output_gradients[layer_position_index], value_output_gradients[layer_position_index], lengths))
        squares = jnp.sum(gradients * gradients, axis=1)
        damping = 0.1 * jnp.sum(squares) / EXAMPLES + 1e-6
        targets = validation[layer_position_index].astype(jnp.float32)
        products = jnp.dot(gradients, targets.T, precision=highest)
        weights = products / (damping + squares[:, None])
        directions = jnp.dot(weights.T, gradients, precision=highest)
        inner = products - jnp.dot(gradients, directions.T, precision=highest) / EXAMPLES
        scores = scores - inner / damping
    return scores
```

```python
import functools

import jax
import jax.numpy as jnp
from jax import lax
from jax.experimental import pallas as pl
from jax.experimental.pallas import tpu as pltpu
from jax.sharding import PartitionSpec as P

F32 = jnp.float32
BF16 = jnp.bfloat16
NN = (((1,), (0,)), ((), ()))
NT = (((1,), (1,)), ((), ()))
LANES = 128
VMEM_BYTES = 40 * 1024 * 1024


def general_local(inputs, grad_key, grad_value, key_down, key_up, value_down, value_up, validation, lengths):
    highest = lax.Precision.HIGHEST
    num_layers, local_examples, seq_slots, _ = inputs.shape
    total_count = lax.axis_size("ex") * local_examples
    low_rank = key_down.shape[1]
    token_mask = (
        lax.broadcasted_iota(jnp.int32, (local_examples, seq_slots), 1) < lengths[:, None]
    ).astype(F32)
    dot = functools.partial(jnp.einsum, preferred_element_type=F32)

    def masked(values):
        return (values * token_mask[None, :, :, None]).astype(BF16)

    z_key = masked(dot("lesd,lrd->lesr", inputs, key_down))
    z_value = masked(dot("lesd,lrd->lesr", inputs, value_down))
    y_key = masked(dot("leso,lor->lesr", grad_key, key_up))
    y_value = masked(dot("leso,lor->lesr", grad_value, value_up))
    pieces = [
        dot("lesr,lesd->lerd", y_key, inputs),
        dot("lesr,leso->lero", z_key, grad_key),
        dot("lesr,lesd->lerd", y_value, inputs),
        dot("lesr,leso->lero", z_value, grad_value),
    ]
    gradients = jnp.concatenate(pieces, axis=3).reshape(num_layers, local_examples, -1)
    squares = jnp.sum(gradients * gradients, axis=2)
    damping = 0.1 * lax.psum(jnp.sum(squares, axis=1), "ex") / total_count + 1e-06
    targets = lax.all_gather(validation, "ex", axis=2, tiled=True).astype(F32)
    products = jnp.einsum("lep,lvp->lev", gradients, targets, precision=highest)
    weights = products / (damping[:, None, None] + squares[:, :, None])
    directions = jnp.einsum("lev,lep->lvp", weights, gradients, precision=highest)
    summed = lax.psum(directions, "ex")
    correction = jnp.einsum("lep,lvp->lev", gradients, summed, precision=highest)
    inner = products - correction / total_count
    return -jnp.sum(inner / damping[:, None, None], axis=0)


CORE, Y, Z1, Z2 = 1, 2, 4, 8
ORDERS = ((Y, Z1), (Z1, Y))


def slot_bits(layer, position):
    first, second = ORDERS[layer]
    return (position >> 2 & 1) * first + (position >> 1 & 1) * second + (position & 1) * Z2


def swap(values, bit):
    size = lax.axis_size("ex")
    return lax.ppermute(values, "ex", [(index, index ^ bit) for index in range(size)])


def fold_lanes(values):
    tiles = [values[:, at : at + LANES] for at in range(0, values.shape[1], LANES)]
    while len(tiles) > 1:
        tiles = [sum(tiles[at : at + 2]) for at in range(0, len(tiles), 2)]
    return tiles[0]


def gradient_kernel(
    scalars, x_ref, gk_ref, gv_ref, ak_ref, av_ref, bk_ref, bv_ref, own_ref, other_ref, square_ref, *, chunk
):
    layer, example = pl.program_id(0), pl.program_id(1)
    index = scalars[0]
    rank = ak_ref.shape[1]
    seq, width = x_ref.shape[2:]
    narrow = gk_ref.shape[3]
    half = rank // 2
    row = lax.broadcasted_iota(jnp.int32, (2 * rank, 2 * rank), 0)
    column = lax.broadcasted_iota(jnp.int32, (2 * rank, 2 * rank), 1)
    position = row % half
    high, low, last = position // 4, position // 2 % 2, position % 2
    is_first = (layer == 0).astype(jnp.int32)
    first_bit = ORDERS[0][0] * is_first + ORDERS[1][0] * (1 - is_first)
    second_bit = ORDERS[0][1] * is_first + ORDERS[1][1] * (1 - is_first)
    relative = high * first_bit + low * second_bit + last * Z2 + row // half % 2
    wanted = jnp.bitwise_xor(relative, jnp.broadcast_to(index, relative.shape)) + row // rank * rank
    order = (column == wanted).astype(F32).astype(BF16)
    mask = (lax.broadcasted_iota(jnp.int32, (1, seq), 1) < scalars[1 + example]).astype(F32)

    def finish(values):
        rounded = (values * mask).astype(BF16)
        return lax.dot_general(order, rounded, NN, preferred_element_type=F32).astype(BF16)

    factor = jnp.concatenate([ak_ref[0], av_ref[0]], axis=0)
    z = finish(lax.dot_general(factor, x_ref[0, 0], NT, preferred_element_type=F32))
    y_key = lax.dot_general(bk_ref[0], gk_ref[0, 0], NT, preferred_element_type=F32)
    y_value = lax.dot_general(bv_ref[0], gv_ref[0, 0], NT, preferred_element_type=F32)
    y = finish(jnp.concatenate([y_key, y_value], axis=0))
    total = jnp.zeros((half, LANES), F32)

    def store(values, at):
        columns = values.shape[1]
        own_ref[0, 0, :, at : at + columns] = values[:half]
        other_ref[0, 0, :, at : at + columns] = values[half:]
        squared = values * values
        return fold_lanes(squared[:half] + squared[half:])

    for at in range(0, width, chunk):
        down = lax.dot_general(y, x_ref[0, 0, :, at : at + chunk], NN, preferred_element_type=F32)
        total += store(down[:rank], at)
        total += store(down[rank:], width + narrow + at)
    up_key = lax.dot_general(z[:rank], gk_ref[0, 0], NN, preferred_element_type=F32)
    total += store(up_key, width)
    up_value = lax.dot_general(z[rank:], gv_ref[0, 0], NN, preferred_element_type=F32)
    total += store(up_value, 2 * width + narrow)
    square_ref[0, 0] = total


def gradients_of(scalars, inputs, grad_key, grad_value, key_down, key_up, value_down, value_up):
    layers, examples, seq, width = inputs.shape
    narrow = grad_key.shape[3]
    rank = key_down.shape[1]
    half = rank // 2
    row_width = 2 * (width + narrow)
    per_example = lambda layer, example, _: (layer, example, 0, 0)
    per_layer = lambda layer, example, _: (layer, 0, 0)
    grad_spec = pl.BlockSpec((1, 1, seq, narrow), per_example)
    down_spec = pl.BlockSpec((1, rank, width), per_layer)
    up_spec = pl.BlockSpec((1, rank, narrow), per_layer)
    row_spec = pl.BlockSpec((1, 1, half, row_width), per_example)
    rows = jax.ShapeDtypeStruct((layers, examples, half, row_width), F32)
    return pl.pallas_call(
        functools.partial(gradient_kernel, chunk=1024),
        grid_spec=pltpu.PrefetchScalarGridSpec(
            num_scalar_prefetch=1,
            grid=(layers, examples),
            in_specs=[
                pl.BlockSpec((1, 1, seq, width), per_example),
                grad_spec,
                grad_spec,
                down_spec,
                down_spec,
                up_spec,
                up_spec,
            ],
            out_specs=[row_spec, row_spec, pl.BlockSpec((1, 1, half, LANES), per_example)],
        ),
        out_shape=[rows, rows, jax.ShapeDtypeStruct((layers, examples, half, LANES), F32)],
        compiler_params=pltpu.CompilerParams(vmem_limit_bytes=VMEM_BYTES),
        cost_estimate=pl.CostEstimate(flops=1 << 32, bytes_accessed=1 << 24, transcendentals=0),
        name="gradients",
    )(
        scalars,
        inputs,
        grad_key,
        grad_value,
        key_down,
        value_down,
        jnp.swapaxes(key_up, 1, 2),
        jnp.swapaxes(value_up, 1, 2),
    )


def dots_kernel(own_ref, received_ref, *refs, sources):
    target_refs, out_ref, rows, total = refs[:-3], refs[-3], refs[-2], refs[-1]
    at = 0
    for ref in target_refs:
        values = ref[...].reshape(ref.shape[-2:]).astype(F32)
        count = values.shape[0] // 2
        rows[0, at : at + count] = values[:count]
        rows[1, at : at + count] = values[count:]
        at += count
    parts = []
    for ref in (own_ref, received_ref):
        for example in range(2):
            gradient = ref[0, example]
            for target in range(2):
                parts.append(fold_lanes(gradient * rows[target]))

    @pl.when(pl.program_id(0) == 0)
    def _():
        total[...] = jnp.zeros_like(total)

    for number, part in enumerate(parts):
        total[number] += part

    @pl.when(pl.program_id(0) == pl.num_programs(0) - 1)
    def _():
        out_ref[...] = jnp.sum(total[...], axis=1)


def dots_of(layer, own, received, targets, columns):
    _, examples, half, row_width = own.shape
    row_spec = pl.BlockSpec((1, examples, half, columns), lambda at: (layer, 0, 0, at))
    specs = []
    for target in targets:
        if target.ndim == 3:
            specs.append(pl.BlockSpec((1, target.shape[1], columns), lambda at: (layer, 0, at)))
        else:
            specs.append(pl.BlockSpec((target.shape[0], columns), lambda at: (0, at)))
    return pl.pallas_call(
        functools.partial(dots_kernel, sources=len(targets)),
        grid=(row_width // columns,),
        in_specs=[row_spec, row_spec] + specs,
        out_specs=pl.BlockSpec((4 * examples, LANES), lambda at: (0, 0)),
        out_shape=jax.ShapeDtypeStruct((4 * examples, LANES), F32),
        scratch_shapes=[pltpu.VMEM((2, half, columns), F32), pltpu.VMEM((4 * examples, half, LANES), F32)],
        compiler_params=pltpu.CompilerParams(vmem_limit_bytes=VMEM_BYTES),
        cost_estimate=pl.CostEstimate(flops=1 << 22, bytes_accessed=3 << 20, transcendentals=0),
        name="dots",
    )(own, received, *targets)


def directions_kernel(
    products_ref, pair_ref, squares_ref, pair_squares_ref, norms_ref, own_ref, received_ref, keep_ref, send_ref, *, count, layer
):
    mine, pair = products_ref[...], pair_ref[...]
    half = mine.shape[0] // 2
    products = mine + jnp.concatenate([pair[half:], pair[:half]], axis=0)
    damping = 0.1 * jnp.sum(norms_ref[layer : layer + 1], axis=1, keepdims=True) / count + 1e-06
    parts = [None, None]
    for number in range(4):
        source = squares_ref if number < 2 else pair_squares_ref
        row = 2 * layer + number % 2
        square = jnp.sum(source[row : row + 1], axis=1, keepdims=True)
        gradient = (own_ref if number < 2 else received_ref)[0, number % 2]
        for target in range(2):
            at = 2 * number + target
            weight = jnp.sum(products[at : at + 1], axis=1, keepdims=True) / (damping + square)
            term = weight * gradient
            parts[target] = term if parts[target] is None else parts[target] + term
    for block, ref in enumerate((keep_ref, send_ref)):
        pieces = []
        for at in (4 * block, 4 * block + 2):
            pieces += [parts[0][at : at + 2], parts[1][at : at + 2]]
        ref[...] = jnp.concatenate(pieces, axis=0).astype(ref.dtype)


def directions_of(layer, products, pair, squares, pair_squares, norms, own, received, count, columns):
    _, examples, half, row_width = own.shape
    row_spec = pl.BlockSpec((1, examples, half, columns), lambda at: (layer, 0, 0, at))
    out_spec = pl.BlockSpec((half, columns), lambda at: (0, at))
    whole = [pl.BlockSpec(array.shape, lambda at: (0, 0)) for array in (products, pair, squares, pair_squares, norms)]
    return pl.pallas_call(
        functools.partial(directions_kernel, count=count, layer=layer),
        grid=(row_width // columns,),
        in_specs=whole + [row_spec, row_spec],
        out_specs=[out_spec, out_spec],
        out_shape=[
            jax.ShapeDtypeStruct((half, row_width), F32),
            jax.ShapeDtypeStruct((half, row_width), BF16),
        ],
        compiler_params=pltpu.CompilerParams(vmem_limit_bytes=VMEM_BYTES),
        cost_estimate=pl.CostEstimate(flops=1 << 22, bytes_accessed=3 << 20, transcendentals=0),
        name="directions",
    )(products, pair, squares, pair_squares, norms, own, received)


def halve_kernel(keep_ref, arrived_ref, rest_ref, send_ref):
    total = keep_ref[...] + arrived_ref[...].astype(F32)
    rest_ref[...] = total[:4]
    send_ref[...] = total[4:].astype(BF16)


def turn_kernel(keep_ref, arrived_ref, rest_ref, send_ref):
    total = keep_ref[...] + arrived_ref[...].astype(F32)
    rest_ref[...] = total
    send_ref[...] = jnp.concatenate([total[1:2], total[0:1], total[3:4], total[2:3]], axis=0).astype(BF16)


def add_call(kernel, keep, arrived, rows):
    width = keep.shape[1]
    return pl.pallas_call(
        kernel,
        out_shape=[jax.ShapeDtypeStruct((rows, width), F32), jax.ShapeDtypeStruct((rows, width), BF16)],
        compiler_params=pltpu.CompilerParams(vmem_limit_bytes=VMEM_BYTES),
        cost_estimate=pl.CostEstimate(flops=1 << 18, bytes_accessed=1 << 20, transcendentals=0),
        name="add",
    )(keep, arrived)


def paired_local(inputs, grad_key, grad_value, key_down, key_up, value_down, value_up, validation, lengths):
    layers, examples = inputs.shape[:2]
    count = lax.axis_size("ex") * examples
    index = lax.axis_index("ex").astype(jnp.int32)
    columns = 4608

    targets = {0: validation}
    for bit in (Y, Z1, Z2):
        targets[bit] = swap(validation, bit)
    scalars = jnp.concatenate([index[None], lengths])
    own, other, square_parts = gradients_of(
        scalars, inputs, grad_key, grad_value, key_down, key_up, value_down, value_up
    )
    received = swap(other, CORE)
    targets[Y | Z1] = swap(targets[Z1], Y)
    targets[Y | Z2] = swap(targets[Z2], Y)
    targets[Z1 | Z2] = swap(targets[Z2], Z1)
    targets[Y | Z1 | Z2] = swap(targets[Z1 | Z2], Y)

    squares = jnp.sum(square_parts, axis=2).reshape(layers * examples, LANES)
    pair_squares = swap(squares, CORE)
    norms = jnp.sum((squares + pair_squares).reshape(layers, examples, LANES), axis=1)
    for bit in (Y, Z1, Z2):
        norms = norms + swap(norms, bit)

    products, corrections = [], []
    for layer in range(layers):
        ordered = [targets[slot_bits(layer, position)] for position in range(8)]
        products.append(dots_of(layer, own, received, ordered, columns))
    pairs = [swap(value, CORE) for value in products]
    for layer, (first, second) in enumerate(ORDERS):
        keep, send = directions_of(
            layer, products[layer], pairs[layer], squares, pair_squares, norms, own, received, count, columns
        )
        keep, send = add_call(halve_kernel, keep, swap(send, first), 4)
        keep, send = add_call(turn_kernel, keep, swap(send, second), 4)
        block = (keep + swap(send, Z2).astype(F32)).astype(BF16)
        from_second = swap(block, second)
        blocks = [block, from_second, swap(block, first), swap(from_second, first)]
        corrections.append(dots_of(layer, own, received, blocks, columns))
    mine = jnp.stack(products) - jnp.stack(corrections) / count
    split = 2 * examples
    inner = mine[:, :split] + swap(mine[:, split:], CORE)
    damping = 0.1 * jnp.sum(norms, axis=1) / count + 1e-06
    scores = -jnp.sum(jnp.sum(inner, axis=2) / damping[:, None], axis=0)
    return scores.reshape(examples, 2)


def solution(mesh):
    in_specs = (
        P(None, ("groups", "ex"), None, None),
        P(None, ("groups", "ex"), None, None),
        P(None, ("groups", "ex"), None, None),
        P(),
        P(),
        P(),
        P(),
        P(None, "groups", "ex"),
        P(("groups", "ex")),
    )
    out_specs = P(("groups", "ex"), None)

    def local(*arguments):
        low_rank = arguments[3].shape[1]
        paired = lax.axis_size("ex") == low_rank == 16 and arguments[0].shape[:2] == (2, 2)
        return (paired_local if paired else general_local)(*arguments)

    return jax.shard_map(local, mesh=mesh, in_specs=in_specs, out_specs=out_specs, check_vma=False)
```

```python
import functools

import jax
import jax.numpy as jnp
from jax import lax
from jax.experimental import pallas as pl
from jax.experimental.pallas import tpu as pltpu
from jax.sharding import PartitionSpec as P

F32 = jnp.float32
BF16 = jnp.bfloat16
NN = (((1,), (0,)), ((), ()))
NT = (((1,), (1,)), ((), ()))
LANES = 128
GRADIENT_VMEM = 18 * 1024 * 1024
SMALL_VMEM = 6 * 1024 * 1024


def general_local(inputs, grad_key, grad_value, key_down, key_up, value_down, value_up, validation, lengths):
    highest = lax.Precision.HIGHEST
    num_layers, local_examples, seq_slots, _ = inputs.shape
    total_count = lax.axis_size("ex") * local_examples
    low_rank = key_down.shape[1]
    token_mask = (
        lax.broadcasted_iota(jnp.int32, (local_examples, seq_slots), 1) < lengths[:, None]
    ).astype(F32)
    dot = functools.partial(jnp.einsum, preferred_element_type=F32)

    def masked(values):
        return (values * token_mask[None, :, :, None]).astype(BF16)

    z_key = masked(dot("lesd,lrd->lesr", inputs, key_down))
    z_value = masked(dot("lesd,lrd->lesr", inputs, value_down))
    y_key = masked(dot("leso,lor->lesr", grad_key, key_up))
    y_value = masked(dot("leso,lor->lesr", grad_value, value_up))
    pieces = [
        dot("lesr,lesd->lerd", y_key, inputs),
        dot("lesr,leso->lero", z_key, grad_key),
        dot("lesr,lesd->lerd", y_value, inputs),
        dot("lesr,leso->lero", z_value, grad_value),
    ]
    gradients = jnp.concatenate(pieces, axis=3).reshape(num_layers, local_examples, -1)
    squares = jnp.sum(gradients * gradients, axis=2)
    damping = 0.1 * lax.psum(jnp.sum(squares, axis=1), "ex") / total_count + 1e-06
    targets = lax.all_gather(validation, "ex", axis=2, tiled=True).astype(F32)
    products = jnp.einsum("lep,lvp->lev", gradients, targets, precision=highest)
    weights = products / (damping[:, None, None] + squares[:, :, None])
    directions = jnp.einsum("lev,lep->lvp", weights, gradients, precision=highest)
    summed = lax.psum(directions, "ex")
    correction = jnp.einsum("lep,lvp->lev", gradients, summed, precision=highest)
    inner = products - correction / total_count
    return -jnp.sum(inner / damping[:, None, None], axis=0)


CORE, Y, Z1, Z2 = 1, 2, 4, 8
ORDERS = ((Y, Z1), (Z1, Y))


def slot_bits(layer, position):
    first, second = ORDERS[layer]
    return (position >> 2 & 1) * first + (position >> 1 & 1) * second + (position & 1) * Z2


def swap(values, bit):
    size = lax.axis_size("ex")
    return lax.ppermute(values, "ex", [(index, index ^ bit) for index in range(size)])


def fold_lanes(values):
    tiles = [values[:, at : at + LANES] for at in range(0, values.shape[1], LANES)]
    while len(tiles) > 1:
        tiles = [sum(tiles[at : at + 2]) for at in range(0, len(tiles), 2)]
    return tiles[0]


def gradient_kernel(
    index_ref, lengths_ref, x_hbm, gk_hbm, gv_hbm, ak_hbm, av_hbm, bk_hbm, bv_hbm, *refs, layer, after, chunk
):
    own_ref, other_ref, square_ref, x_ref, gk_ref, gv_ref, a_ref, b_ref, semaphores = refs[after:]
    examples, seq, width = x_ref.shape
    narrow = gk_ref.shape[2]
    rank = bk_hbm.shape[1]
    half = rank // 2
    copies = {}

    def start(name, source, target):
        copies[name] = pltpu.make_async_copy(source, target, semaphores.at[len(copies)])
        copies[name].start()

    start("bk", bk_hbm.at[layer], b_ref.at[0])
    start("bv", bv_hbm.at[layer], b_ref.at[1])
    start("gk", gk_hbm.at[layer], gk_ref)
    start("gv", gv_hbm.at[layer], gv_ref)
    start("ak", ak_hbm.at[layer], a_ref.at[0])
    start("av", av_hbm.at[layer], a_ref.at[1])
    for at in range(0, width, chunk):
        columns = pl.ds(at, chunk)
        start(("x", at), x_hbm.at[layer, :, :, columns], x_ref.at[:, :, columns])

    row = lax.broadcasted_iota(jnp.int32, (2 * rank, 2 * rank), 0)
    column = lax.broadcasted_iota(jnp.int32, (2 * rank, 2 * rank), 1)
    position = row % half
    first_bit, second_bit = ORDERS[layer]
    relative = position // 4 * first_bit + position // 2 % 2 * second_bit + position % 2 * Z2 + row // half % 2
    wanted = jnp.bitwise_xor(relative, jnp.broadcast_to(index_ref[0], relative.shape)) + row // rank * rank
    order = (column == wanted).astype(F32).astype(BF16)
    token = lax.broadcasted_iota(jnp.int32, (1, examples * seq), 1)
    mask = jnp.zeros(token.shape, F32)
    for example in range(examples):
        inside = (token >= example * seq) & (token < example * seq + lengths_ref[example])
        mask = jnp.where(inside, 1.0, mask)
    own_tokens = [slice(example * seq, (example + 1) * seq) for example in range(examples)]
    totals = [jnp.zeros((half, LANES), F32) for _ in range(examples)]

    def finish(values):
        rounded = (values * mask).astype(BF16)
        return lax.dot_general(order, rounded, NN, preferred_element_type=F32).astype(BF16)

    def store(example, values, at):
        columns = values.shape[1]
        own_ref[example, :, at : at + columns] = values[:half]
        other_ref[example, :, at : at + columns] = values[half:]
        squared = values * values
        totals[example] += fold_lanes(squared[:half] + squared[half:])

    for name in ("bk", "bv", "gk", "gv"):
        copies[name].wait()
    grad_key = gk_ref[...].reshape(examples * seq, narrow)
    grad_value = gv_ref[...].reshape(examples * seq, narrow)
    y_key = lax.dot_general(b_ref[0], grad_key, NT, preferred_element_type=F32)
    y_value = lax.dot_general(b_ref[1], grad_value, NT, preferred_element_type=F32)
    y = finish(jnp.concatenate([y_key, y_value], axis=0))
    copies["ak"].wait()
    copies["av"].wait()
    z = jnp.zeros((2 * rank, examples * seq), F32)
    for at in range(0, width, chunk):
        copies["x", at].wait()
        columns = slice(at, at + chunk)
        x = x_ref[:, :, columns].reshape(examples * seq, chunk)
        factor = jnp.concatenate([a_ref[0, :, columns], a_ref[1, :, columns]], axis=0)
        z += lax.dot_general(factor, x, NT, preferred_element_type=F32)
        for example, tokens in enumerate(own_tokens):
            down = lax.dot_general(y[:, tokens], x_ref[example, :, columns], NN, preferred_element_type=F32)
            store(example, down[:rank], at)
            store(example, down[rank:], width + narrow + at)
    z = finish(z)
    for example, tokens in enumerate(own_tokens):
        up_key = lax.dot_general(z[:rank, tokens], gk_ref[example], NN, preferred_element_type=F32)
        store(example, up_key, width)
        up_value = lax.dot_general(z[rank:, tokens], gv_ref[example], NN, preferred_element_type=F32)
        store(example, up_value, 2 * width + narrow)
        square_ref[example : example + 1] = jnp.sum(totals[example], axis=0, keepdims=True)


IN_VMEM = pl.BlockSpec(memory_space=pltpu.VMEM)
ANYWHERE = pl.BlockSpec(memory_space=pl.ANY)
COLUMNS = 1024


def in_hbm(array):
    return pltpu.with_memory_space_constraint(array, pltpu.HBM)


def gradients_of(layer, index, lengths, inputs, grad_key, grad_value, key_down, key_up, value_down, value_up, after=()):
    _, examples, seq, width = inputs.shape
    narrow = grad_key.shape[3]
    rank = key_down.shape[1]
    row_width = 2 * (width + narrow)
    chunk = 2048
    copies = 6 + width // chunk
    rows = jax.ShapeDtypeStruct((examples, rank // 2, row_width), F32)
    return pl.pallas_call(
        functools.partial(gradient_kernel, layer=layer, after=len(after), chunk=chunk),
        in_specs=[pl.BlockSpec(memory_space=pltpu.SMEM)] * 2 + [ANYWHERE] * (7 + len(after)),
        out_specs=[IN_VMEM] * 3,
        out_shape=[rows, rows, jax.ShapeDtypeStruct((examples, LANES), F32)],
        scratch_shapes=[
            pltpu.VMEM((examples, seq, width), BF16),
            pltpu.VMEM((examples, seq, narrow), BF16),
            pltpu.VMEM((examples, seq, narrow), BF16),
            pltpu.VMEM((2, rank, width), BF16),
            pltpu.VMEM((2, rank, narrow), BF16),
            pltpu.SemaphoreType.DMA((copies,)),
        ],
        compiler_params=pltpu.CompilerParams(vmem_limit_bytes=GRADIENT_VMEM),
        cost_estimate=pl.CostEstimate(flops=1 << 32, bytes_accessed=1 << 24, transcendentals=0),
        name="gradients",
    )(
        index,
        lengths,
        in_hbm(inputs),
        in_hbm(grad_key),
        in_hbm(grad_value),
        in_hbm(key_down),
        in_hbm(value_down),
        in_hbm(jnp.swapaxes(key_up, 1, 2)),
        in_hbm(jnp.swapaxes(value_up, 1, 2)),
        *after,
    )


def chunks(ref):
    def run(body, init):
        def step(number, carry):
            return body(pl.ds(pl.multiple_of(number * COLUMNS, COLUMNS), COLUMNS), carry)

        return lax.fori_loop(0, ref.shape[-1] // COLUMNS, step, init)

    return run


def dots_kernel(*refs, layers, groups, started):
    out_ref = refs[-1]
    at = 2 * layers
    for layer in range(layers):
        own_ref, received_ref = refs[2 * layer : 2 * layer + 2]
        target_refs = refs[at : at + len(groups[layer])]
        at += len(groups[layer])
        slots = own_ref.shape[1]

        def body(columns, totals):
            pieces, filled = ([], []), 0
            for start, ref in sorted(zip(groups[layer], target_refs), key=lambda pair: pair[0]):
                index = (layer, slice(None), columns) if len(ref.shape) == 3 else (slice(None), columns)
                values = ref[index].astype(F32)
                count = values.shape[0] // 2
                for target in range(2):
                    if start > filled:
                        pieces[target].append(jnp.zeros((start - filled, values.shape[1]), F32))
                    pieces[target].append(values[target * count : (target + 1) * count])
                filled = start + count
            if filled < slots:
                for target in range(2):
                    pieces[target].append(jnp.zeros((slots - filled, COLUMNS), F32))
            rows = [jnp.concatenate(group, axis=0) for group in pieces]
            updated = []
            for number, total in enumerate(totals):
                gradient = (own_ref if number < 4 else received_ref)[number // 2 % 2, :, columns]
                updated.append(total + fold_lanes(gradient * rows[number % 2]))
            return tuple(updated)

        zero = jnp.zeros((slots, LANES), F32)
        totals = chunks(own_ref)(body, (zero,) * 8)
        for number, total in enumerate(totals):
            row = layer * 8 + number
            value = jnp.sum(total, axis=0, keepdims=True)
            out_ref[row : row + 1] = value + refs[-2][row : row + 1] if started else value


def dots_of(rows, targets, start=None):
    layers = len(rows)
    flat = [array for pair in rows for array in pair] + [array for group in targets for array in group.values()]
    flat += [] if start is None else [start]
    return pl.pallas_call(
        functools.partial(
            dots_kernel, layers=layers, groups=[tuple(group) for group in targets], started=start is not None
        ),
        in_specs=[IN_VMEM] * len(flat),
        out_specs=IN_VMEM,
        out_shape=jax.ShapeDtypeStruct((8 * layers, LANES), F32),
        compiler_params=pltpu.CompilerParams(vmem_limit_bytes=SMALL_VMEM),
        cost_estimate=pl.CostEstimate(flops=1 << 22, bytes_accessed=3 << 20, transcendentals=0),
        name="dots",
    )(*flat)


def directions_kernel(
    products_ref, pair_ref, squares_ref, pair_squares_ref, norm_ref, own_ref, received_ref, keep_ref, send_ref, *, count, layer
):
    mine, pair = products_ref[8 * layer : 8 * layer + 8], pair_ref[8 * layer : 8 * layer + 8]
    products = mine + jnp.concatenate([pair[4:], pair[:4]], axis=0)
    damping = 0.1 * jnp.sum(norm_ref[layer : layer + 1], axis=1, keepdims=True) / count + 1e-06
    weights = []
    for number in range(4):
        source = squares_ref if number < 2 else pair_squares_ref
        row = 2 * layer + number % 2
        scale = damping + jnp.sum(source[row : row + 1], axis=1, keepdims=True)
        for target in range(2):
            at = 2 * number + target
            weights.append(jnp.sum(products[at : at + 1], axis=1, keepdims=True) / scale)

    def body(columns, carry):
        gradients = [ref[example, :, columns] for ref in (own_ref, received_ref) for example in range(2)]
        parts = [sum(weights[2 * number + target] * gradients[number] for number in range(4)) for target in range(2)]
        for block, ref in enumerate((keep_ref, send_ref)):
            pieces = []
            for at in (4 * block, 4 * block + 2):
                pieces += [parts[0][at : at + 2], parts[1][at : at + 2]]
            ref[:, columns] = jnp.concatenate(pieces, axis=0).astype(ref.dtype)
        return carry

    chunks(own_ref)(body, 0)


def directions_of(layer, products, pair, squares, pair_squares, norms, own, received, count):
    _, half, row_width = own.shape
    return pl.pallas_call(
        functools.partial(directions_kernel, count=count, layer=layer),
        in_specs=[IN_VMEM] * 7,
        out_specs=[IN_VMEM] * 2,
        out_shape=[
            jax.ShapeDtypeStruct((half, row_width), F32),
            jax.ShapeDtypeStruct((half, row_width), BF16),
        ],
        compiler_params=pltpu.CompilerParams(vmem_limit_bytes=SMALL_VMEM),
        cost_estimate=pl.CostEstimate(flops=1 << 22, bytes_accessed=3 << 20, transcendentals=0),
        name="directions",
    )(products, pair, squares, pair_squares, norms, own, received)


def halve_kernel(keep_ref, arrived_ref, rest_ref, send_ref):
    total = keep_ref[...] + arrived_ref[...].astype(F32)
    rest_ref[...] = total[:4]
    send_ref[...] = total[4:].astype(BF16)


def turn_kernel(keep_ref, arrived_ref, rest_ref, send_ref):
    total = keep_ref[...] + arrived_ref[...].astype(F32)
    rest_ref[...] = total
    send_ref[...] = jnp.concatenate([total[1:2], total[0:1], total[3:4], total[2:3]], axis=0).astype(BF16)


def add_call(kernel, keep, arrived, rows):
    width = keep.shape[1]
    return pl.pallas_call(
        kernel,
        out_shape=[jax.ShapeDtypeStruct((rows, width), F32), jax.ShapeDtypeStruct((rows, width), BF16)],
        compiler_params=pltpu.CompilerParams(vmem_limit_bytes=SMALL_VMEM),
        cost_estimate=pl.CostEstimate(flops=1 << 18, bytes_accessed=1 << 20, transcendentals=0),
        name="add",
    )(keep, arrived)


def paired_local(inputs, grad_key, grad_value, key_down, key_up, value_down, value_up, validation, lengths):
    layers, examples = inputs.shape[:2]
    count = lax.axis_size("ex") * examples
    index = lax.axis_index("ex").astype(jnp.int32)[None]
    arguments = (index, lengths, inputs, grad_key, grad_value, key_down, key_up, value_down, value_up)

    targets = {0: validation}
    for bit in (Z2, Y, Z1):
        targets[bit] = swap(validation, bit)
    rows, parts = [], []
    for layer in range(layers):
        after = [targets[bit] for bit in (Z2, Y, Z1)] if layer else []
        own, other, square_parts = gradients_of(layer, *arguments, after=after)
        rows.append((own, swap(other, CORE)))
        parts.append(square_parts)
    targets[Y | Z2] = swap(targets[Z2], Y)
    targets[Z1 | Z2] = swap(targets[Z2], Z1)
    targets[Y | Z1] = swap(targets[Z1], Y)
    targets[Y | Z1 | Z2] = swap(targets[Y | Z2], Z1)

    squares = jnp.concatenate(parts)
    pair_squares = swap(squares, CORE)
    norms = squares + pair_squares
    norms = jnp.stack([norms[0] + norms[1], norms[2] + norms[3]])
    for bit in (Y, Z1, Z2):
        norms = norms + swap(norms, bit)

    slots = [[slot_bits(layer, position) for position in range(8)] for layer in range(layers)]
    early = [{at: targets[slot] for at, slot in enumerate(row) if slot != Y | Z1 | Z2} for row in slots]
    late = [{at: targets[slot] for at, slot in enumerate(row) if slot == Y | Z1 | Z2} for row in slots]
    products = dots_of(rows, late, dots_of(rows, early))
    pair = swap(products, CORE)
    early, late = [], []
    for layer, (first, second) in enumerate(ORDERS):
        keep, send = directions_of(layer, products, pair, squares, pair_squares, norms, *rows[layer], count)
        keep, send = add_call(halve_kernel, keep, swap(send, first), 4)
        keep, send = add_call(turn_kernel, keep, swap(send, second), 4)
        block = (keep + swap(send, Z2).astype(F32)).astype(BF16)
        from_second = swap(block, second)
        early.append({0: block, 2: from_second, 4: swap(block, first)})
        late.append({6: swap(from_second, first)})
    corrections = dots_of(rows, late, dots_of(rows, early))
    mine = (products - corrections / count).reshape(layers, 4 * examples, LANES)
    split = 2 * examples
    inner = mine[:, :split] + swap(mine[:, split:], CORE)
    damping = 0.1 * jnp.sum(norms, axis=1) / count + 1e-06
    scores = -jnp.sum(jnp.sum(inner, axis=2) / damping[:, None], axis=0)
    return scores.reshape(examples, 2)


def solution(mesh):
    in_specs = (
        P(None, ("groups", "ex"), None, None),
        P(None, ("groups", "ex"), None, None),
        P(None, ("groups", "ex"), None, None),
        P(),
        P(),
        P(),
        P(),
        P(None, "groups", "ex"),
        P(("groups", "ex")),
    )
    out_specs = P(("groups", "ex"), None)

    def local(*arguments):
        low_rank = arguments[3].shape[1]
        paired = lax.axis_size("ex") == low_rank == 16 and arguments[0].shape[:2] == (2, 2)
        return (paired_local if paired else general_local)(*arguments)

    return jax.shard_map(local, mesh=mesh, in_specs=in_specs, out_specs=out_specs, check_vma=False)
```

```python
import functools

import jax
import jax.numpy as jnp
from jax import lax
from jax.experimental import pallas as pl
from jax.experimental.pallas import tpu as pltpu
from jax.sharding import PartitionSpec as P

F32 = jnp.float32
BF16 = jnp.bfloat16
NN = (((1,), (0,)), ((), ()))
NT = (((1,), (1,)), ((), ()))
LANES = 128
GRADIENT_VMEM = 18 * 1024 * 1024
SMALL_VMEM = 6 * 1024 * 1024


def general_local(inputs, grad_key, grad_value, key_down, key_up, value_down, value_up, validation, lengths):
    highest = lax.Precision.HIGHEST
    num_layers, local_examples, seq_slots, _ = inputs.shape
    total_count = lax.axis_size("ex") * local_examples
    low_rank = key_down.shape[1]
    token_mask = (
        lax.broadcasted_iota(jnp.int32, (local_examples, seq_slots), 1) < lengths[:, None]
    ).astype(F32)
    dot = functools.partial(jnp.einsum, preferred_element_type=F32)

    def masked(values):
        return (values * token_mask[None, :, :, None]).astype(BF16)

    z_key = masked(dot("lesd,lrd->lesr", inputs, key_down))
    z_value = masked(dot("lesd,lrd->lesr", inputs, value_down))
    y_key = masked(dot("leso,lor->lesr", grad_key, key_up))
    y_value = masked(dot("leso,lor->lesr", grad_value, value_up))
    pieces = [
        dot("lesr,lesd->lerd", y_key, inputs),
        dot("lesr,leso->lero", z_key, grad_key),
        dot("lesr,lesd->lerd", y_value, inputs),
        dot("lesr,leso->lero", z_value, grad_value),
    ]
    gradients = jnp.concatenate(pieces, axis=3).reshape(num_layers, local_examples, -1)
    squares = jnp.sum(gradients * gradients, axis=2)
    damping = 0.1 * lax.psum(jnp.sum(squares, axis=1), "ex") / total_count + 1e-06
    targets = lax.all_gather(validation, "ex", axis=2, tiled=True).astype(F32)
    products = jnp.einsum("lep,lvp->lev", gradients, targets, precision=highest)
    weights = products / (damping[:, None, None] + squares[:, :, None])
    directions = jnp.einsum("lev,lep->lvp", weights, gradients, precision=highest)
    summed = lax.psum(directions, "ex")
    correction = jnp.einsum("lep,lvp->lev", gradients, summed, precision=highest)
    inner = products - correction / total_count
    return -jnp.sum(inner / damping[:, None, None], axis=0)


CORE, Y, Z1, Z2 = 1, 2, 4, 8
ORDERS = ((Y, Z1), (Z1, Y))


def slot_bits(layer, position):
    first, second = ORDERS[layer]
    return (position >> 2 & 1) * first + (position >> 1 & 1) * second + (position & 1) * Z2


def swap(values, bit):
    size = lax.axis_size("ex")
    return lax.ppermute(values, "ex", [(index, index ^ bit) for index in range(size)])


def fold_lanes(values):
    tiles = [values[:, at : at + LANES] for at in range(0, values.shape[1], LANES)]
    while len(tiles) > 1:
        tiles = [sum(tiles[at : at + 2]) for at in range(0, len(tiles), 2)]
    return tiles[0]


def rank_order(index, layer, rank):
    half = rank // 2
    row = lax.broadcasted_iota(jnp.int32, (2 * rank, 2 * rank), 0)
    column = lax.broadcasted_iota(jnp.int32, (2 * rank, 2 * rank), 1)
    position = row % half
    first_bit, second_bit = ORDERS[layer]
    relative = position // 4 * first_bit + position // 2 % 2 * second_bit + position % 2 * Z2 + row // half % 2
    wanted = jnp.bitwise_xor(relative, jnp.broadcast_to(index, relative.shape)) + row // rank * rank
    return (column == wanted).astype(F32).astype(BF16)


def ordered(order, key, value):
    both = jnp.concatenate([key, value], axis=0)
    return lax.dot_general(order, both, NN, preferred_element_type=F32).astype(BF16)


class Unit:
    def __init__(self, number, length, up_factor, gk, gv, outputs):
        self.number, self.gk, self.gv = number, gk, gv
        self.own_ref, self.other_ref, self.square_ref = outputs
        self.seq, self.narrow = gk.shape
        self.rank = up_factor.shape[0] // 2
        token = lax.broadcasted_iota(jnp.int32, (1, self.seq), 1)
        self.mask = (token < length).astype(F32)
        y_key = lax.dot_general(up_factor[: self.rank], gk, NT, preferred_element_type=F32)
        y_value = lax.dot_general(up_factor[self.rank :], gv, NT, preferred_element_type=F32)
        self.y = (jnp.concatenate([y_key, y_value], axis=0) * self.mask).astype(BF16)
        self.z = jnp.zeros((2 * self.rank, self.seq), F32)
        self.total = jnp.zeros((self.rank // 2, LANES), F32)

    def store(self, values, at):
        columns, half = values.shape[1], self.rank // 2
        self.own_ref[self.number, :, at : at + columns] = values[:half]
        self.other_ref[self.number, :, at : at + columns] = values[half:]
        squared = values * values
        self.total += fold_lanes(squared[:half] + squared[half:])

    def chunk(self, factor, x, at, width):
        self.z += lax.dot_general(factor, x, NT, preferred_element_type=F32)
        down = lax.dot_general(self.y, x, NN, preferred_element_type=F32)
        self.store(down[: self.rank], at)
        self.store(down[self.rank :], width + self.narrow + at)

    def finish(self, width):
        z = (self.z * self.mask).astype(BF16)
        self.store(lax.dot_general(z[: self.rank], self.gk, NN, preferred_element_type=F32), width)
        up_value = lax.dot_general(z[self.rank :], self.gv, NN, preferred_element_type=F32)
        self.store(up_value, 2 * width + self.narrow)
        self.square_ref[self.number : self.number + 1] = jnp.sum(self.total, axis=0, keepdims=True)


def first_gradients_kernel(
    index_ref, lengths_ref, x_hbm, gk_hbm, gv_hbm, ak_hbm, av_hbm, bk_hbm, bv_hbm, *refs, chunk
):
    outputs, (x_last, gk_last, gv_last, factor_last, up_last) = refs[:3], refs[3:8]
    x_ref, gk_ref, gv_ref, a_ref, b_ref, semaphores = refs[8:]
    rank, width = a_ref.shape[2:]
    copies = {}

    def start(name, source, target):
        copies[name] = pltpu.make_async_copy(source, target, semaphores.at[len(copies)])
        copies[name].start()

    def wait(*names):
        for name in names:
            copies[name].wait()

    for layer in range(2):
        start(("bk", layer), bk_hbm.at[layer], b_ref.at[layer, 0])
        start(("bv", layer), bv_hbm.at[layer], b_ref.at[layer, 1])
        if layer == 0:
            start(("gk", 0), gk_hbm.at[0], gk_ref.at[0:2])
            start(("gv", 0), gv_hbm.at[0], gv_ref.at[0:2])
        else:
            start(("gk", 1), gk_hbm.at[1, 0], gk_ref.at[2])
            start(("gv", 1), gv_hbm.at[1, 0], gv_ref.at[2])
        start(("ak", layer), ak_hbm.at[layer], a_ref.at[layer, 0])
        start(("av", layer), av_hbm.at[layer], a_ref.at[layer, 1])
        if layer == 0:
            for at in range(0, width, chunk):
                columns = pl.ds(at, chunk)
                start(("x", at), x_hbm.at[0, :, :, columns], x_ref.at[0:2, :, columns])
        else:
            start("x", x_hbm.at[1, 0], x_ref.at[2])
    start("gk", gk_hbm.at[1, 1], gk_last)
    start("gv", gv_hbm.at[1, 1], gv_last)
    start("x last", x_hbm.at[1, 1], x_last)

    order = rank_order(index_ref[0], 0, rank)
    wait(("bk", 0), ("bv", 0), ("gk", 0), ("gv", 0))
    up_factor = ordered(order, b_ref[0, 0], b_ref[0, 1])
    units = [Unit(number, lengths_ref[number], up_factor, gk_ref[number], gv_ref[number], outputs) for number in range(2)]
    wait(("ak", 0), ("av", 0))
    for at in range(0, width, chunk):
        columns = slice(at, at + chunk)
        factor = ordered(order, a_ref[0, 0, :, columns], a_ref[0, 1, :, columns])
        wait(("x", at))
        for unit in units:
            unit.chunk(factor, x_ref[unit.number, :, columns], at, width)
    for unit in units:
        unit.finish(width)

    order = rank_order(index_ref[0], 1, rank)
    wait(("bk", 1), ("bv", 1), ("gk", 1), ("gv", 1), ("ak", 1), ("av", 1), "x")
    up_factor = ordered(order, b_ref[1, 0], b_ref[1, 1])
    up_last[...] = up_factor
    unit = Unit(2, lengths_ref[0], up_factor, gk_ref[2], gv_ref[2], outputs)
    for at in range(0, width, chunk):
        columns = slice(at, at + chunk)
        factor = ordered(order, a_ref[1, 0, :, columns], a_ref[1, 1, :, columns])
        factor_last[:, columns] = factor
        unit.chunk(factor, x_ref[2, :, columns], at, width)
    unit.finish(width)
    wait("gk", "gv", "x last")


def last_gradients_kernel(lengths_ref, x_ref, gk_ref, gv_ref, factor_ref, up_ref, *refs, chunk):
    width = x_ref.shape[1]
    unit = Unit(3, lengths_ref[1], up_ref[...], gk_ref[...], gv_ref[...], refs[-3:])
    for at in range(0, width, chunk):
        columns = slice(at, at + chunk)
        unit.chunk(factor_ref[:, columns], x_ref[:, columns], at, width)
    unit.finish(width)


IN_VMEM = pl.BlockSpec(memory_space=pltpu.VMEM)
IN_SMEM = pl.BlockSpec(memory_space=pltpu.SMEM)
ANYWHERE = pl.BlockSpec(memory_space=pl.ANY)
COLUMNS = 1024
SQUARES, NORMS = 16, 20


def in_hbm(array):
    return pltpu.with_memory_space_constraint(array, pltpu.HBM)


def gradients_of(index, lengths, inputs, grad_key, grad_value, key_down, key_up, value_down, value_up, after):
    _, _, seq, width = inputs.shape
    narrow = grad_key.shape[3]
    rank = key_down.shape[1]
    rows = jax.ShapeDtypeStruct((4, rank // 2, 2 * (width + narrow)), F32)
    outputs = [rows, rows, jax.ShapeDtypeStruct((4, LANES), F32)]
    lengths = in_hbm(lengths)
    parameters = pltpu.CompilerParams(vmem_limit_bytes=GRADIENT_VMEM)
    *results, x, gk, gv, factor, up_factor = pl.pallas_call(
        functools.partial(first_gradients_kernel, chunk=2048),
        in_specs=[IN_SMEM] * 2 + [ANYWHERE] * 7,
        out_specs=[IN_VMEM] * 8,
        out_shape=outputs
        + [
            jax.ShapeDtypeStruct(shape, BF16)
            for shape in ((seq, width), (seq, narrow), (seq, narrow), (2 * rank, width), (2 * rank, narrow))
        ],
        scratch_shapes=[
            pltpu.VMEM((3, seq, width), BF16),
            pltpu.VMEM((3, seq, narrow), BF16),
            pltpu.VMEM((3, seq, narrow), BF16),
            pltpu.VMEM((2, 2, rank, width), BF16),
            pltpu.VMEM((2, 2, rank, narrow), BF16),
            pltpu.SemaphoreType.DMA((20,)),
        ],
        compiler_params=parameters,
        cost_estimate=pl.CostEstimate(flops=1 << 32, bytes_accessed=1 << 24, transcendentals=0),
        name="first_gradients",
    )(
        index,
        lengths,
        in_hbm(inputs),
        in_hbm(grad_key),
        in_hbm(grad_value),
        in_hbm(key_down),
        in_hbm(value_down),
        in_hbm(jnp.swapaxes(key_up, 1, 2)),
        in_hbm(jnp.swapaxes(value_up, 1, 2)),
    )
    return pl.pallas_call(
        functools.partial(last_gradients_kernel, chunk=2048),
        in_specs=[IN_SMEM] + [IN_VMEM] * 8 + [ANYWHERE] * len(after),
        out_specs=[IN_VMEM] * 3,
        out_shape=outputs,
        input_output_aliases={6: 0, 7: 1, 8: 2},
        compiler_params=parameters,
        cost_estimate=pl.CostEstimate(flops=1 << 30, bytes_accessed=1 << 22, transcendentals=0),
        name="last_gradients",
    )(lengths, x, gk, gv, factor, up_factor, *results, *after)


def example_of(refs, layer, number):
    return refs[number // 2], 2 * layer + number % 2


def chunks(ref):
    def run(body, init):
        def step(number, carry):
            return body(pl.ds(pl.multiple_of(number * COLUMNS, COLUMNS), COLUMNS), carry)

        return lax.fori_loop(0, ref.shape[-1] // COLUMNS, step, init)

    return run


def dots_kernel(*refs, layers, groups, extras):
    out_ref, extra_refs = refs[-1], refs[-1 - extras : -1]
    start_ref, tables = (extra_refs[0], extra_refs[1:]) if extras else (None, ())
    slots = refs[0].shape[1]
    at = 2
    for layer in range(layers):
        target_refs = refs[at : at + len(groups[layer])]
        at += len(groups[layer])
        examples = [example_of(refs, layer, number) for number in range(4)]

        def body(columns, totals):
            pieces, filled = ([], []), 0
            for start, ref in sorted(zip(groups[layer], target_refs), key=lambda pair: pair[0]):
                index = (layer, slice(None), columns) if len(ref.shape) == 3 else (slice(None), columns)
                values = ref[index].astype(F32)
                count = values.shape[0] // 2
                for target in range(2):
                    if start > filled:
                        pieces[target].append(jnp.zeros((start - filled, values.shape[1]), F32))
                    pieces[target].append(values[target * count : (target + 1) * count])
                filled = start + count
            if filled < slots:
                for target in range(2):
                    pieces[target].append(jnp.zeros((slots - filled, COLUMNS), F32))
            rows = [jnp.concatenate(group, axis=0) for group in pieces]
            updated = []
            for number, total in enumerate(totals):
                ref, place = examples[number // 2]
                updated.append(total + fold_lanes(ref[place, :, columns] * rows[number % 2]))
            return tuple(updated)

        zero = jnp.zeros((slots, LANES), F32)
        totals = chunks(refs[0])(body, (zero,) * 8)
        for number, total in enumerate(totals):
            row = layer * 8 + number
            value = jnp.sum(total, axis=0, keepdims=True)
            out_ref[row : row + 1] = value + start_ref[row : row + 1] if start_ref is not None else value
    if tables:
        squares_ref, norms_ref, arrived_ref = tables
        out_ref[SQUARES:NORMS] = squares_ref[...]
        out_ref[NORMS:] = norms_ref[...] + arrived_ref[...]


def dots_of(rows, targets, extras=()):
    layers = len(targets)
    flat = [*rows] + [array for group in targets for array in group.values()] + [*extras]
    out_rows = NORMS + layers if len(extras) > 1 else SQUARES
    return pl.pallas_call(
        functools.partial(
            dots_kernel, layers=layers, groups=[tuple(group) for group in targets], extras=len(extras)
        ),
        in_specs=[IN_VMEM] * len(flat),
        out_specs=IN_VMEM,
        out_shape=jax.ShapeDtypeStruct((out_rows, LANES), F32),
        compiler_params=pltpu.CompilerParams(vmem_limit_bytes=SMALL_VMEM),
        cost_estimate=pl.CostEstimate(flops=1 << 22, bytes_accessed=3 << 20, transcendentals=0),
        name="dots",
    )(*flat)


def directions_kernel(mine_ref, pair_ref, *refs, count, layer):
    keep_ref, send_ref = refs[2:]
    mine, pair = mine_ref[8 * layer : 8 * layer + 8], pair_ref[8 * layer : 8 * layer + 8]
    products = mine + jnp.concatenate([pair[4:], pair[:4]], axis=0)
    row = NORMS + layer
    norm = mine_ref[row : row + 1] + pair_ref[row : row + 1]
    damping = 0.1 * jnp.sum(norm, axis=1, keepdims=True) / count + 1e-06
    weights = []
    for number in range(4):
        source = mine_ref if number < 2 else pair_ref
        row = SQUARES + 2 * layer + number % 2
        scale = damping + jnp.sum(source[row : row + 1], axis=1, keepdims=True)
        for target in range(2):
            at = 2 * number + target
            weights.append(jnp.sum(products[at : at + 1], axis=1, keepdims=True) / scale)
    examples = [example_of(refs, layer, number) for number in range(4)]

    def body(columns, carry):
        gradients = [ref[place, :, columns] for ref, place in examples]
        parts = [sum(weights[2 * number + target] * gradients[number] for number in range(4)) for target in range(2)]
        for block, ref in enumerate((keep_ref, send_ref)):
            pieces = []
            for at in (4 * block, 4 * block + 2):
                pieces += [parts[0][at : at + 2], parts[1][at : at + 2]]
            ref[:, columns] = jnp.concatenate(pieces, axis=0).astype(ref.dtype)
        return carry

    chunks(keep_ref)(body, 0)


def directions_of(layer, mine, pair, rows, count):
    _, half, row_width = rows[0].shape
    return pl.pallas_call(
        functools.partial(directions_kernel, count=count, layer=layer),
        in_specs=[IN_VMEM] * 4,
        out_specs=[IN_VMEM] * 2,
        out_shape=[
            jax.ShapeDtypeStruct((half, row_width), F32),
            jax.ShapeDtypeStruct((half, row_width), BF16),
        ],
        compiler_params=pltpu.CompilerParams(vmem_limit_bytes=SMALL_VMEM),
        cost_estimate=pl.CostEstimate(flops=1 << 22, bytes_accessed=3 << 20, transcendentals=0),
        name="directions",
    )(mine, pair, *rows)


def halve_kernel(keep_ref, arrived_ref, rest_ref, send_ref):
    total = keep_ref[...] + arrived_ref[...].astype(F32)
    rest_ref[...] = total[:4]
    send_ref[...] = total[4:].astype(BF16)


def turn_kernel(keep_ref, arrived_ref, rest_ref, send_ref):
    total = keep_ref[...] + arrived_ref[...].astype(F32)
    rest_ref[...] = total
    send_ref[...] = jnp.concatenate([total[1:2], total[0:1], total[3:4], total[2:3]], axis=0).astype(BF16)


def add_call(kernel, keep, arrived, rows):
    width = keep.shape[1]
    return pl.pallas_call(
        kernel,
        out_shape=[jax.ShapeDtypeStruct((rows, width), F32), jax.ShapeDtypeStruct((rows, width), BF16)],
        compiler_params=pltpu.CompilerParams(vmem_limit_bytes=SMALL_VMEM),
        cost_estimate=pl.CostEstimate(flops=1 << 18, bytes_accessed=1 << 20, transcendentals=0),
        name="add",
    )(keep, arrived)


def paired_local(inputs, grad_key, grad_value, key_down, key_up, value_down, value_up, validation, lengths):
    layers, examples = inputs.shape[:2]
    count = lax.axis_size("ex") * examples
    index = lax.axis_index("ex").astype(jnp.int32)[None]
    arguments = (index, lengths, inputs, grad_key, grad_value, key_down, key_up, value_down, value_up)

    targets = {0: validation}
    first_bits = (Z2, Y, Z1, Y | Z1)
    for bits in first_bits:
        targets[bits] = swap(validation, bits)
    own, other, squares = gradients_of(*arguments, after=[targets[bits] for bits in first_bits])
    rows = (own, swap(other, CORE))
    for bits in (Y, Z1):
        targets[bits | Z2] = swap(targets[Z2], bits)
    targets[Y | Z1 | Z2] = swap(targets[Y | Z2], Z1)

    norms = jnp.stack([squares[0] + squares[1], squares[2] + squares[3]])
    for bit in (Y, Z1):
        norms = norms + swap(norms, bit)
    arrived = swap(norms, Z2)

    slots = [[slot_bits(layer, position) for position in range(8)] for layer in range(layers)]
    early = [{at: targets[bits] for at, bits in enumerate(row) if bits in (0, *first_bits)} for row in slots]
    late = [{at: targets[bits] for at, bits in enumerate(row) if bits not in (0, *first_bits)} for row in slots]
    mine = dots_of(rows, late, [dots_of(rows, early), squares, norms, arrived])
    pair = swap(mine, CORE)
    early, late = [], []
    for layer, (first, second) in enumerate(ORDERS):
        keep, send = directions_of(layer, mine, pair, rows, count)
        keep, send = add_call(halve_kernel, keep, swap(send, first), 4)
        keep, send = add_call(turn_kernel, keep, swap(send, second), 4)
        block = (keep + swap(send, Z2).astype(F32)).astype(BF16)
        from_second = swap(block, second)
        early.append({0: block, 2: from_second})
        late.append({4: swap(block, first), 6: swap(from_second, first)})
    corrections = dots_of(rows, late, [dots_of(rows, early)])
    damping = 0.1 * jnp.sum(mine[NORMS:] + pair[NORMS:], axis=1) / count + 1e-06
    inner = (mine[:SQUARES] - corrections / count).reshape(layers, 4 * examples, LANES)
    split = 2 * examples
    inner = inner[:, :split] + swap(inner[:, split:], CORE)
    scores = -jnp.sum(jnp.sum(inner, axis=2) / damping[:, None], axis=0)
    return scores.reshape(examples, 2)


def solution(mesh):
    in_specs = (
        P(None, ("groups", "ex"), None, None),
        P(None, ("groups", "ex"), None, None),
        P(None, ("groups", "ex"), None, None),
        P(),
        P(),
        P(),
        P(),
        P(None, "groups", "ex"),
        P(("groups", "ex")),
    )
    out_specs = P(("groups", "ex"), None)

    def local(*arguments):
        low_rank = arguments[3].shape[1]
        paired = lax.axis_size("ex") == low_rank == 16 and arguments[0].shape[:2] == (2, 2)
        return (paired_local if paired else general_local)(*arguments)

    return jax.shard_map(local, mesh=mesh, in_specs=in_specs, out_specs=out_specs, check_vma=False)
```

```python
import functools

import jax
import jax.numpy as jnp
from jax import lax
from jax.experimental import pallas as pl
from jax.experimental.pallas import tpu as pltpu
from jax.sharding import PartitionSpec as P

F32 = jnp.float32
BF16 = jnp.bfloat16
NN = (((1,), (0,)), ((), ()))
NT = (((1,), (1,)), ((), ()))
LANES = 128
GRADIENT_VMEM = 18 * 1024 * 1024
SMALL_VMEM = 6 * 1024 * 1024


def general_local(inputs, grad_key, grad_value, key_down, key_up, value_down, value_up, validation, lengths):
    highest = lax.Precision.HIGHEST
    num_layers, local_examples, seq_slots, _ = inputs.shape
    total_count = lax.axis_size("ex") * local_examples
    low_rank = key_down.shape[1]
    token_mask = (
        lax.broadcasted_iota(jnp.int32, (local_examples, seq_slots), 1) < lengths[:, None]
    ).astype(F32)
    dot = functools.partial(jnp.einsum, preferred_element_type=F32)

    def masked(values):
        return (values * token_mask[None, :, :, None]).astype(BF16)

    z_key = masked(dot("lesd,lrd->lesr", inputs, key_down))
    z_value = masked(dot("lesd,lrd->lesr", inputs, value_down))
    y_key = masked(dot("leso,lor->lesr", grad_key, key_up))
    y_value = masked(dot("leso,lor->lesr", grad_value, value_up))
    pieces = [
        dot("lesr,lesd->lerd", y_key, inputs),
        dot("lesr,leso->lero", z_key, grad_key),
        dot("lesr,lesd->lerd", y_value, inputs),
        dot("lesr,leso->lero", z_value, grad_value),
    ]
    gradients = jnp.concatenate(pieces, axis=3).reshape(num_layers, local_examples, -1)
    squares = jnp.sum(gradients * gradients, axis=2)
    damping = 0.1 * lax.psum(jnp.sum(squares, axis=1), "ex") / total_count + 1e-06
    targets = lax.all_gather(validation, "ex", axis=2, tiled=True).astype(F32)
    products = jnp.einsum("lep,lvp->lev", gradients, targets, precision=highest)
    weights = products / (damping[:, None, None] + squares[:, :, None])
    directions = jnp.einsum("lev,lep->lvp", weights, gradients, precision=highest)
    summed = lax.psum(directions, "ex")
    correction = jnp.einsum("lep,lvp->lev", gradients, summed, precision=highest)
    inner = products - correction / total_count
    return -jnp.sum(inner / damping[:, None, None], axis=0)


CORE, Y, Z1, Z2 = 1, 2, 4, 8
ORDERS = ((Y, Z1), (Z1, Y))


def slot_bits(layer, position):
    first, second = ORDERS[layer]
    return (position >> 2 & 1) * first + (position >> 1 & 1) * second + (position & 1) * Z2


def swap(values, bit):
    size = lax.axis_size("ex")
    return lax.ppermute(values, "ex", [(index, index ^ bit) for index in range(size)])


def fold_lanes(values):
    tiles = [values[:, at : at + LANES] for at in range(0, values.shape[1], LANES)]
    while len(tiles) > 1:
        tiles = [sum(tiles[at : at + 2]) for at in range(0, len(tiles), 2)]
    return tiles[0]


def rank_order(index, layer, rank):
    half = rank // 2
    row = lax.broadcasted_iota(jnp.int32, (2 * rank, 2 * rank), 0)
    column = lax.broadcasted_iota(jnp.int32, (2 * rank, 2 * rank), 1)
    position = row % half
    first_bit, second_bit = ORDERS[layer]
    relative = position // 4 * first_bit + position // 2 % 2 * second_bit + position % 2 * Z2 + row // half % 2
    wanted = jnp.bitwise_xor(relative, jnp.broadcast_to(index, relative.shape)) + row // rank * rank
    return (column == wanted).astype(F32).astype(BF16)


def ordered(order, key, value):
    both = jnp.concatenate([key, value], axis=0)
    return lax.dot_general(order, both, NN, preferred_element_type=F32).astype(BF16)


class Unit:
    def __init__(self, number, length, up_factor, gk, gv, outputs):
        self.number, self.gk, self.gv = number, gk, gv
        self.own_ref, self.other_ref, self.square_ref = outputs
        self.seq, self.narrow = gk.shape
        self.rank = up_factor.shape[0] // 2
        token = lax.broadcasted_iota(jnp.int32, (1, self.seq), 1)
        self.mask = (token < length).astype(F32)
        y_key = lax.dot_general(up_factor[: self.rank], gk, NT, preferred_element_type=F32)
        y_value = lax.dot_general(up_factor[self.rank :], gv, NT, preferred_element_type=F32)
        self.y = (jnp.concatenate([y_key, y_value], axis=0) * self.mask).astype(BF16)
        self.z = jnp.zeros((2 * self.rank, self.seq), F32)
        self.total = jnp.zeros((self.rank // 2, LANES), F32)

    def store(self, values, at):
        columns, half = values.shape[1], self.rank // 2
        self.own_ref[self.number, :, at : at + columns] = values[:half]
        self.other_ref[self.number, :, at : at + columns] = values[half:]
        squared = values * values
        self.total += fold_lanes(squared[:half] + squared[half:])

    def chunk(self, factor, x, at, width):
        self.z += lax.dot_general(factor, x, NT, preferred_element_type=F32)
        down = lax.dot_general(self.y, x, NN, preferred_element_type=F32)
        self.store(down[: self.rank], at)
        self.store(down[self.rank :], width + self.narrow + at)

    def finish(self, width):
        z = (self.z * self.mask).astype(BF16)
        self.store(lax.dot_general(z[: self.rank], self.gk, NN, preferred_element_type=F32), width)
        up_value = lax.dot_general(z[self.rank :], self.gv, NN, preferred_element_type=F32)
        self.store(up_value, 2 * width + self.narrow)
        self.square_ref[self.number : self.number + 1] = jnp.sum(self.total, axis=0, keepdims=True)


def first_gradients_kernel(
    index_ref, lengths_ref, x_hbm, gk_hbm, gv_hbm, ak_hbm, av_hbm, bk_hbm, bv_hbm, *refs, chunk
):
    outputs, (x_last, gk_last, gv_last, factor_last, up_last) = refs[:3], refs[3:8]
    x_ref, gk_ref, gv_ref, a_ref, b_ref, semaphores = refs[8:]
    rank, width = a_ref.shape[2:]
    copies = {}

    def start(name, source, target):
        copies[name] = pltpu.make_async_copy(source, target, semaphores.at[len(copies)])
        copies[name].start()

    def wait(*names):
        for name in names:
            copies[name].wait()

    for layer in range(2):
        start(("bk", layer), bk_hbm.at[layer], b_ref.at[layer, 0])
        start(("bv", layer), bv_hbm.at[layer], b_ref.at[layer, 1])
        if layer == 0:
            start(("gk", 0), gk_hbm.at[0], gk_ref.at[0:2])
            start(("gv", 0), gv_hbm.at[0], gv_ref.at[0:2])
        else:
            start(("gk", 1), gk_hbm.at[1, 0], gk_ref.at[2])
            start(("gv", 1), gv_hbm.at[1, 0], gv_ref.at[2])
        start(("ak", layer), ak_hbm.at[layer], a_ref.at[layer, 0])
        start(("av", layer), av_hbm.at[layer], a_ref.at[layer, 1])
        if layer == 0:
            for at in range(0, width, chunk):
                columns = pl.ds(at, chunk)
                start(("x", at), x_hbm.at[0, :, :, columns], x_ref.at[0:2, :, columns])
        else:
            start("x", x_hbm.at[1, 0], x_ref.at[2])
    start("gk", gk_hbm.at[1, 1], gk_last)
    start("gv", gv_hbm.at[1, 1], gv_last)
    start("x last", x_hbm.at[1, 1], x_last)

    order = rank_order(index_ref[0], 0, rank)
    wait(("bk", 0), ("bv", 0), ("gk", 0), ("gv", 0))
    up_factor = ordered(order, b_ref[0, 0], b_ref[0, 1])
    units = [Unit(number, lengths_ref[number], up_factor, gk_ref[number], gv_ref[number], outputs) for number in range(2)]
    wait(("ak", 0), ("av", 0))
    for at in range(0, width, chunk):
        columns = slice(at, at + chunk)
        factor = ordered(order, a_ref[0, 0, :, columns], a_ref[0, 1, :, columns])
        wait(("x", at))
        for unit in units:
            unit.chunk(factor, x_ref[unit.number, :, columns], at, width)
    for unit in units:
        unit.finish(width)

    order = rank_order(index_ref[0], 1, rank)
    wait(("bk", 1), ("bv", 1), ("gk", 1), ("gv", 1), ("ak", 1), ("av", 1), "x")
    up_factor = ordered(order, b_ref[1, 0], b_ref[1, 1])
    up_last[...] = up_factor
    unit = Unit(2, lengths_ref[0], up_factor, gk_ref[2], gv_ref[2], outputs)
    for at in range(0, width, chunk):
        columns = slice(at, at + chunk)
        factor = ordered(order, a_ref[1, 0, :, columns], a_ref[1, 1, :, columns])
        factor_last[:, columns] = factor
        unit.chunk(factor, x_ref[2, :, columns], at, width)
    unit.finish(width)
    wait("gk", "gv", "x last")


def last_gradients_kernel(lengths_ref, x_ref, gk_ref, gv_ref, factor_ref, up_ref, *refs, chunk):
    width = x_ref.shape[1]
    unit = Unit(3, lengths_ref[1], up_ref[...], gk_ref[...], gv_ref[...], refs[-3:])
    for at in range(0, width, chunk):
        columns = slice(at, at + chunk)
        unit.chunk(factor_ref[:, columns], x_ref[:, columns], at, width)
    unit.finish(width)


IN_VMEM = pl.BlockSpec(memory_space=pltpu.VMEM)
IN_SMEM = pl.BlockSpec(memory_space=pltpu.SMEM)
ANYWHERE = pl.BlockSpec(memory_space=pl.ANY)
COLUMNS = 1024
SQUARES, NORMS = 16, 20


def in_hbm(array):
    return pltpu.with_memory_space_constraint(array, pltpu.HBM)


def gradients_of(index, lengths, inputs, grad_key, grad_value, key_down, key_up, value_down, value_up, after):
    _, _, seq, width = inputs.shape
    narrow = grad_key.shape[3]
    rank = key_down.shape[1]
    rows = jax.ShapeDtypeStruct((4, rank // 2, 2 * (width + narrow)), F32)
    outputs = [rows, rows, jax.ShapeDtypeStruct((4, LANES), F32)]
    lengths = in_hbm(lengths)
    parameters = pltpu.CompilerParams(vmem_limit_bytes=GRADIENT_VMEM)
    *results, x, gk, gv, factor, up_factor = pl.pallas_call(
        functools.partial(first_gradients_kernel, chunk=2048),
        in_specs=[IN_SMEM] * 2 + [ANYWHERE] * 7,
        out_specs=[IN_VMEM] * 8,
        out_shape=outputs
        + [
            jax.ShapeDtypeStruct(shape, BF16)
            for shape in ((seq, width), (seq, narrow), (seq, narrow), (2 * rank, width), (2 * rank, narrow))
        ],
        scratch_shapes=[
            pltpu.VMEM((3, seq, width), BF16),
            pltpu.VMEM((3, seq, narrow), BF16),
            pltpu.VMEM((3, seq, narrow), BF16),
            pltpu.VMEM((2, 2, rank, width), BF16),
            pltpu.VMEM((2, 2, rank, narrow), BF16),
            pltpu.SemaphoreType.DMA((20,)),
        ],
        compiler_params=parameters,
        cost_estimate=pl.CostEstimate(flops=1 << 32, bytes_accessed=1 << 24, transcendentals=0),
        name="first_gradients",
    )(
        index,
        lengths,
        in_hbm(inputs),
        in_hbm(grad_key),
        in_hbm(grad_value),
        in_hbm(key_down),
        in_hbm(value_down),
        in_hbm(jnp.swapaxes(key_up, 1, 2)),
        in_hbm(jnp.swapaxes(value_up, 1, 2)),
    )
    return pl.pallas_call(
        functools.partial(last_gradients_kernel, chunk=2048),
        in_specs=[IN_SMEM] + [IN_VMEM] * 8 + [ANYWHERE] * len(after),
        out_specs=[IN_VMEM] * 3,
        out_shape=outputs,
        input_output_aliases={6: 0, 7: 1, 8: 2},
        compiler_params=parameters,
        cost_estimate=pl.CostEstimate(flops=1 << 30, bytes_accessed=1 << 22, transcendentals=0),
        name="last_gradients",
    )(lengths, x, gk, gv, factor, up_factor, *results, *after)


def example_of(refs, layer, number):
    return refs[number // 2], 2 * layer + number % 2


def chunks(ref):
    def run(body, init):
        def step(number, carry):
            return body(pl.ds(pl.multiple_of(number * COLUMNS, COLUMNS), COLUMNS), carry)

        return lax.fori_loop(0, ref.shape[-1] // COLUMNS, step, init)

    return run


def dots_kernel(*refs, groups, extras):
    out_ref, extra_refs = refs[-1], refs[-1 - extras : -1]
    start_ref, tables = (extra_refs[0], extra_refs[1:]) if extras else (None, ())
    slots = refs[0].shape[1]
    at = 2
    for place, (layer, starts) in enumerate(groups):
        target_refs = refs[at : at + len(starts)]
        at += len(starts)
        examples = [example_of(refs, layer, number) for number in range(4)]

        def body(columns, totals):
            pieces, filled = ([], []), 0
            for start, ref in sorted(zip(starts, target_refs), key=lambda pair: pair[0]):
                index = (layer, slice(None), columns) if len(ref.shape) == 3 else (slice(None), columns)
                values = ref[index].astype(F32)
                count = values.shape[0] // 2
                for target in range(2):
                    if start > filled:
                        pieces[target].append(jnp.zeros((start - filled, values.shape[1]), F32))
                    pieces[target].append(values[target * count : (target + 1) * count])
                filled = start + count
            if filled < slots:
                for target in range(2):
                    pieces[target].append(jnp.zeros((slots - filled, COLUMNS), F32))
            rows = [jnp.concatenate(group, axis=0) for group in pieces]
            updated = []
            for number, total in enumerate(totals):
                ref, place = examples[number // 2]
                updated.append(total + fold_lanes(ref[place, :, columns] * rows[number % 2]))
            return tuple(updated)

        zero = jnp.zeros((slots, LANES), F32)
        totals = chunks(refs[0])(body, (zero,) * 8)
        for number, total in enumerate(totals):
            row = place * 8 + number
            value = jnp.sum(total, axis=0, keepdims=True)
            out_ref[row : row + 1] = value + start_ref[row : row + 1] if start_ref is not None else value
    if tables:
        squares_ref, norms_ref, arrived_ref = tables
        out_ref[SQUARES:NORMS] = squares_ref[...]
        out_ref[NORMS:] = norms_ref[...] + arrived_ref[...]


def dots_of(rows, targets, extras=()):
    flat = [*rows] + [array for group in targets.values() for array in group.values()] + [*extras]
    out_rows = NORMS + len(targets) if len(extras) > 1 else 8 * len(targets)
    groups = [(layer, tuple(group)) for layer, group in targets.items()]
    return pl.pallas_call(
        functools.partial(dots_kernel, groups=groups, extras=len(extras)),
        in_specs=[IN_VMEM] * len(flat),
        out_specs=IN_VMEM,
        out_shape=jax.ShapeDtypeStruct((out_rows, LANES), F32),
        compiler_params=pltpu.CompilerParams(vmem_limit_bytes=SMALL_VMEM),
        cost_estimate=pl.CostEstimate(flops=1 << 22, bytes_accessed=3 << 20, transcendentals=0),
        name="dots",
    )(*flat)


def directions_kernel(mine_ref, pair_ref, *refs, count, layer):
    block_refs = refs[2:]
    mine, pair = mine_ref[8 * layer : 8 * layer + 8], pair_ref[8 * layer : 8 * layer + 8]
    products = mine + jnp.concatenate([pair[4:], pair[:4]], axis=0)
    row = NORMS + layer
    norm = mine_ref[row : row + 1] + pair_ref[row : row + 1]
    damping = 0.1 * jnp.sum(norm, axis=1, keepdims=True) / count + 1e-06
    weights = []
    for number in range(4):
        source = mine_ref if number < 2 else pair_ref
        row = SQUARES + 2 * layer + number % 2
        scale = damping + jnp.sum(source[row : row + 1], axis=1, keepdims=True)
        for target in range(2):
            at = 2 * number + target
            weights.append(jnp.sum(products[at : at + 1], axis=1, keepdims=True) / scale)
    examples = [example_of(refs, layer, number) for number in range(4)]

    def body(columns, carry):
        gradients = [ref[place, :, columns] for ref, place in examples]
        parts = [sum(weights[2 * number + target] * gradients[number] for number in range(4)) for target in range(2)]
        for block, ref in enumerate(block_refs):
            at = 2 * block
            pieces = [parts[0][at : at + 2], parts[1][at : at + 2]]
            ref[:, columns] = jnp.concatenate(pieces, axis=0).astype(ref.dtype)
        return carry

    chunks(block_refs[0])(body, 0)


def directions_of(layer, mine, pair, rows, count):
    _, half, row_width = rows[0].shape
    return pl.pallas_call(
        functools.partial(directions_kernel, count=count, layer=layer),
        in_specs=[IN_VMEM] * 4,
        out_specs=[IN_VMEM] * 4,
        out_shape=[jax.ShapeDtypeStruct((half // 2, row_width), kind) for kind in (F32, BF16, BF16, BF16)],
        compiler_params=pltpu.CompilerParams(vmem_limit_bytes=SMALL_VMEM),
        cost_estimate=pl.CostEstimate(flops=1 << 22, bytes_accessed=3 << 20, transcendentals=0),
        name="directions",
    )(mine, pair, *rows)


def turn_kernel(keep_ref, *refs):
    rest_ref, send_ref = refs[-2:]
    total = keep_ref[...]
    for ref in refs[:-2]:
        total += ref[...].astype(F32)
    rest_ref[...] = total
    send_ref[...] = jnp.concatenate([total[1:2], total[0:1], total[3:4], total[2:3]], axis=0).astype(BF16)


def turned(keep, arrived):
    return pl.pallas_call(
        turn_kernel,
        out_shape=[jax.ShapeDtypeStruct(keep.shape, F32), jax.ShapeDtypeStruct(keep.shape, BF16)],
        compiler_params=pltpu.CompilerParams(vmem_limit_bytes=SMALL_VMEM),
        cost_estimate=pl.CostEstimate(flops=1 << 18, bytes_accessed=1 << 20, transcendentals=0),
        name="add",
    )(keep, *arrived)


def paired_local(inputs, grad_key, grad_value, key_down, key_up, value_down, value_up, validation, lengths):
    layers, examples = inputs.shape[:2]
    count = lax.axis_size("ex") * examples
    index = lax.axis_index("ex").astype(jnp.int32)[None]
    arguments = (index, lengths, inputs, grad_key, grad_value, key_down, key_up, value_down, value_up)

    targets = {0: validation}
    first_bits = (Z2, Y, Z1, Y | Z1)
    for bits in first_bits:
        targets[bits] = swap(validation, bits)
    own, other, squares = gradients_of(*arguments, after=[targets[bits] for bits in first_bits])
    rows = (own, swap(other, CORE))
    for bits in (Y, Z1):
        targets[bits | Z2] = swap(targets[Z2], bits)
    targets[Y | Z1 | Z2] = swap(targets[Y | Z2], Z1)

    norms = jnp.stack([squares[0] + squares[1], squares[2] + squares[3]])
    for bit in (Y, Z1):
        norms = norms + swap(norms, bit)
    arrived = swap(norms, Z2)

    slots = [[slot_bits(layer, position) for position in range(8)] for layer in range(layers)]
    early = {
        layer: {at: targets[bits] for at, bits in enumerate(row) if bits in (0, *first_bits)}
        for layer, row in enumerate(slots)
    }
    late = {
        layer: {at: targets[bits] for at, bits in enumerate(row) if bits not in (0, *first_bits)}
        for layer, row in enumerate(slots)
    }
    mine = dots_of(rows, late, [dots_of(rows, early), squares, norms, arrived])
    pair = swap(mine, CORE)
    corrections = [None] * layers
    for layer in reversed(range(layers)):
        first, second = ORDERS[layer]
        keep, *sends = directions_of(layer, mine, pair, rows, count)
        keep, send = turned(keep, [swap(send, bits) for send, bits in zip(sends, (second, first, first | second))])
        block = (keep + swap(send, Z2).astype(F32)).astype(BF16)
        blocks = {0: block, 2: swap(block, second), 4: swap(block, first), 6: swap(block, first | second)}
        corrections[layer] = dots_of(rows, {layer: blocks})
    damping = 0.1 * jnp.sum(mine[NORMS:] + pair[NORMS:], axis=1) / count + 1e-06
    inner = mine[:SQUARES].reshape(layers, 4 * examples, LANES) - jnp.stack(corrections) / count
    split = 2 * examples
    inner = inner[:, :split] + swap(inner[:, split:], CORE)
    scores = -jnp.sum(jnp.sum(inner, axis=2) / damping[:, None], axis=0)
    return scores.reshape(examples, 2)


def solution(mesh):
    in_specs = (
        P(None, ("groups", "ex"), None, None),
        P(None, ("groups", "ex"), None, None),
        P(None, ("groups", "ex"), None, None),
        P(),
        P(),
        P(),
        P(),
        P(None, "groups", "ex"),
        P(("groups", "ex")),
    )
    out_specs = P(("groups", "ex"), None)

    def local(*arguments):
        low_rank = arguments[3].shape[1]
        paired = lax.axis_size("ex") == low_rank == 16 and arguments[0].shape[:2] == (2, 2)
        return (paired_local if paired else general_local)(*arguments)

    return jax.shard_map(local, mesh=mesh, in_specs=in_specs, out_specs=out_specs, check_vma=False)
```

```python
import functools

import jax
import jax.numpy as jnp
from jax import lax
from jax.experimental import pallas as pl
from jax.experimental.pallas import tpu as pltpu
from jax.sharding import PartitionSpec as P

F32 = jnp.float32
BF16 = jnp.bfloat16
NN = (((1,), (0,)), ((), ()))
NT = (((1,), (1,)), ((), ()))
LANES = 128
GRADIENT_VMEM = 18 * 1024 * 1024
SMALL_VMEM = 6 * 1024 * 1024


def general_local(inputs, grad_key, grad_value, key_down, key_up, value_down, value_up, validation, lengths):
    highest = lax.Precision.HIGHEST
    num_layers, local_examples, seq_slots, _ = inputs.shape
    total_count = lax.axis_size("ex") * local_examples
    low_rank = key_down.shape[1]
    token_mask = (
        lax.broadcasted_iota(jnp.int32, (local_examples, seq_slots), 1) < lengths[:, None]
    ).astype(F32)
    dot = functools.partial(jnp.einsum, preferred_element_type=F32)

    def masked(values):
        return (values * token_mask[None, :, :, None]).astype(BF16)

    z_key = masked(dot("lesd,lrd->lesr", inputs, key_down))
    z_value = masked(dot("lesd,lrd->lesr", inputs, value_down))
    y_key = masked(dot("leso,lor->lesr", grad_key, key_up))
    y_value = masked(dot("leso,lor->lesr", grad_value, value_up))
    pieces = [
        dot("lesr,lesd->lerd", y_key, inputs),
        dot("lesr,leso->lero", z_key, grad_key),
        dot("lesr,lesd->lerd", y_value, inputs),
        dot("lesr,leso->lero", z_value, grad_value),
    ]
    gradients = jnp.concatenate(pieces, axis=3).reshape(num_layers, local_examples, -1)
    squares = jnp.sum(gradients * gradients, axis=2)
    damping = 0.1 * lax.psum(jnp.sum(squares, axis=1), "ex") / total_count + 1e-06
    targets = lax.all_gather(validation, "ex", axis=2, tiled=True).astype(F32)
    products = jnp.einsum("lep,lvp->lev", gradients, targets, precision=highest)
    weights = products / (damping[:, None, None] + squares[:, :, None])
    directions = jnp.einsum("lev,lep->lvp", weights, gradients, precision=highest)
    summed = lax.psum(directions, "ex")
    correction = jnp.einsum("lep,lvp->lev", gradients, summed, precision=highest)
    inner = products - correction / total_count
    return -jnp.sum(inner / damping[:, None, None], axis=0)


CORE, Y, Z1, Z2 = 1, 2, 4, 8
QUAD = (Z1, Y, Y | Z1)
SLOTS = [bits | last for bits in (0, *QUAD) for last in (0, Z2)]


def swap(values, bit):
    size = lax.axis_size("ex")
    return lax.ppermute(values, "ex", [(index, index ^ bit) for index in range(size)])


def fold_lanes(values):
    tiles = [values[:, at : at + LANES] for at in range(0, values.shape[1], LANES)]
    while len(tiles) > 1:
        tiles = [sum(tiles[at : at + 2]) for at in range(0, len(tiles), 2)]
    return tiles[0]


def rank_order(index, rank):
    half = rank // 2
    row = lax.broadcasted_iota(jnp.int32, (2 * rank, 2 * rank), 0)
    column = lax.broadcasted_iota(jnp.int32, (2 * rank, 2 * rank), 1)
    position = row % half
    relative = position // 4 * Y + position // 2 % 2 * Z1 + position % 2 * Z2 + row // half % 2
    wanted = jnp.bitwise_xor(relative, jnp.broadcast_to(index, relative.shape)) + row // rank * rank
    return (column == wanted).astype(F32).astype(BF16)


def ordered(order, key, value):
    both = jnp.concatenate([key, value], axis=0)
    return lax.dot_general(order, both, NN, preferred_element_type=F32).astype(BF16)


class Unit:
    def __init__(self, number, length, up_factor, gk, gv, outputs):
        self.number, self.gk, self.gv = number, gk, gv
        self.own_ref, self.other_ref, self.square_ref = outputs
        self.seq, self.narrow = gk.shape
        self.rank = up_factor.shape[0] // 2
        token = lax.broadcasted_iota(jnp.int32, (1, self.seq), 1)
        self.mask = (token < length).astype(F32)
        y_key = lax.dot_general(up_factor[: self.rank], gk, NT, preferred_element_type=F32)
        y_value = lax.dot_general(up_factor[self.rank :], gv, NT, preferred_element_type=F32)
        self.y = (jnp.concatenate([y_key, y_value], axis=0) * self.mask).astype(BF16)
        self.z = jnp.zeros((2 * self.rank, self.seq), F32)
        self.total = jnp.zeros((self.rank // 2, LANES), F32)

    def store(self, values, at):
        columns, half = values.shape[1], self.rank // 2
        self.own_ref[self.number, :, at : at + columns] = values[:half]
        self.other_ref[self.number, :, at : at + columns] = values[half:]
        squared = values * values
        self.total += fold_lanes(squared[:half] + squared[half:])

    def chunk(self, factor, x, at, width):
        self.z += lax.dot_general(factor, x, NT, preferred_element_type=F32)
        down = lax.dot_general(self.y, x, NN, preferred_element_type=F32)
        self.store(down[: self.rank], at)
        self.store(down[self.rank :], width + self.narrow + at)

    def finish(self, width):
        z = (self.z * self.mask).astype(BF16)
        self.store(lax.dot_general(z[: self.rank], self.gk, NN, preferred_element_type=F32), width)
        up_value = lax.dot_general(z[self.rank :], self.gv, NN, preferred_element_type=F32)
        self.store(up_value, 2 * width + self.narrow)
        self.square_ref[self.number : self.number + 1] = jnp.sum(self.total, axis=0, keepdims=True)


def gradients_kernel(
    index_ref,
    lengths_ref,
    x_hbm,
    gk_hbm,
    gv_hbm,
    ak_hbm,
    av_hbm,
    bk_hbm,
    bv_hbm,
    own_ref,
    other_ref,
    square_ref,
    x_ref,
    gk_ref,
    gv_ref,
    a_ref,
    b_ref,
    semaphores,
    *,
    chunks,
):
    outputs = (own_ref, other_ref, square_ref)
    layers, _, rank, width = a_ref.shape
    examples = x_ref.shape[1]
    copies = {}

    def start(name, source, target):
        copies[name] = pltpu.make_async_copy(source, target, semaphores.at[len(copies)])
        copies[name].start()

    def wait(*names):
        for name in names:
            copies[name].wait()

    for layer in range(layers):
        start(("bk", layer), bk_hbm.at[layer], b_ref.at[layer, 0])
        start(("bv", layer), bv_hbm.at[layer], b_ref.at[layer, 1])
        start(("gk", layer), gk_hbm.at[layer], gk_ref.at[layer])
        start(("gv", layer), gv_hbm.at[layer], gv_ref.at[layer])
        start(("ak", layer), ak_hbm.at[layer], a_ref.at[layer, 0])
        start(("av", layer), av_hbm.at[layer], a_ref.at[layer, 1])
        for at in range(0, width, chunks[layer]):
            columns = pl.ds(at, chunks[layer])
            start(("x", layer, at), x_hbm.at[layer, :, :, columns], x_ref.at[layer, :, :, columns])

    order = rank_order(index_ref[0], rank)
    for layer in range(layers):
        wait(("bk", layer), ("bv", layer), ("gk", layer), ("gv", layer))
        up_factor = ordered(order, b_ref[layer, 0], b_ref[layer, 1])
        units = [
            Unit(layer * examples + at, lengths_ref[at], up_factor, gk_ref[layer, at], gv_ref[layer, at], outputs)
            for at in range(examples)
        ]
        wait(("ak", layer), ("av", layer))
        for at in range(0, width, COLUMNS * 2):
            columns = slice(at, at + COLUMNS * 2)
            factor = ordered(order, a_ref[layer, 0, :, columns], a_ref[layer, 1, :, columns])
            if at % chunks[layer] == 0:
                wait(("x", layer, at))
            for example, unit in enumerate(units):
                unit.chunk(factor, x_ref[layer, example, :, columns], at, width)
        for unit in units:
            unit.finish(width)


def gate_kernel(*refs):
    pass


IN_VMEM = pl.BlockSpec(memory_space=pltpu.VMEM)
IN_SMEM = pl.BlockSpec(memory_space=pltpu.SMEM)
ANYWHERE = pl.BlockSpec(memory_space=pl.ANY)
COLUMNS = 1024
STREAMS = (9216, 9216)
SQUARES, NORMS = 16, 20


def in_hbm(array):
    return pltpu.with_memory_space_constraint(array, pltpu.HBM)


def gradients_of(index, lengths, inputs, grad_key, grad_value, key_down, key_up, value_down, value_up, after):
    _, _, seq, width = inputs.shape
    narrow = grad_key.shape[3]
    rank = key_down.shape[1]
    rows = jax.ShapeDtypeStruct((4, rank // 2, 2 * (width + narrow)), F32)
    outputs = [rows, rows, jax.ShapeDtypeStruct((4, LANES), F32)]
    lengths = in_hbm(lengths)
    parameters = pltpu.CompilerParams(vmem_limit_bytes=GRADIENT_VMEM)
    own, other, squares = pl.pallas_call(
        functools.partial(gradients_kernel, chunks=(2048, 8192)),
        in_specs=[IN_SMEM] * 2 + [ANYWHERE] * 7,
        out_specs=[IN_VMEM] * 3,
        out_shape=outputs,
        scratch_shapes=[
            pltpu.VMEM((2, 2, seq, width), BF16),
            pltpu.VMEM((2, 2, seq, narrow), BF16),
            pltpu.VMEM((2, 2, seq, narrow), BF16),
            pltpu.VMEM((2, 2, rank, width), BF16),
            pltpu.VMEM((2, 2, rank, narrow), BF16),
            pltpu.SemaphoreType.DMA((17,)),
        ],
        compiler_params=parameters,
        cost_estimate=pl.CostEstimate(flops=1 << 32, bytes_accessed=1 << 24, transcendentals=0),
        name="gradients",
    )(
        index,
        lengths,
        in_hbm(inputs),
        in_hbm(grad_key),
        in_hbm(grad_value),
        in_hbm(key_down),
        in_hbm(value_down),
        in_hbm(jnp.swapaxes(key_up, 1, 2)),
        in_hbm(jnp.swapaxes(value_up, 1, 2)),
    )
    other, squares = pl.pallas_call(
        gate_kernel,
        in_specs=[ANYWHERE] * (2 + len(after)),
        out_specs=[ANYWHERE] * 2,
        out_shape=outputs[1:],
        input_output_aliases={0: 0, 1: 1},
        compiler_params=pltpu.CompilerParams(vmem_limit_bytes=SMALL_VMEM),
        cost_estimate=pl.CostEstimate(flops=1 << 10, bytes_accessed=1 << 10, transcendentals=0),
        name="gate",
    )(other, squares, *after)
    return own, other, squares


def example_of(refs, layer, number):
    return refs[number // 2], 2 * layer + number % 2


def chunks(width, body, init):
    def step(number, carry):
        return body(pl.multiple_of(number * COLUMNS, COLUMNS), carry)

    return lax.fori_loop(0, width // COLUMNS, step, init)


def dots_kernel(*refs, starts, offset, width, extras):
    target_refs = refs[2 : 2 + len(starts)]
    out_ref, extra_refs = refs[-1], refs[-1 - extras : -1]
    start_ref, tables = (extra_refs[0], extra_refs[1:]) if extras else (None, ())
    slots = refs[0].shape[1]
    for layer in range(2):

        def body(at, totals):
            pieces, filled = ([], []), 0
            for start, ref in zip(starts, target_refs):
                columns = pl.ds(at, COLUMNS)
                if len(ref.shape) == 3:
                    values = ref[layer, :, columns].astype(F32)
                else:
                    values = ref[4 * layer : 4 * layer + 4, columns].astype(F32)
                count = values.shape[0] // 2
                for target in range(2):
                    if start > filled:
                        pieces[target].append(jnp.zeros((start - filled, COLUMNS), F32))
                    pieces[target].append(values[target * count : (target + 1) * count])
                filled = start + count
            if filled < slots:
                for target in range(2):
                    pieces[target].append(jnp.zeros((slots - filled, COLUMNS), F32))
            rows = [jnp.concatenate(group, axis=0) for group in pieces]
            updated = []
            for number, total in enumerate(totals):
                ref, place = example_of(refs, layer, number // 2)
                gradient = ref[place, :, pl.ds(offset + at, COLUMNS)]
                updated.append(total + fold_lanes(gradient * rows[number % 2]))
            return tuple(updated)

        totals = chunks(width, body, (jnp.zeros((slots, LANES), F32),) * 8)
        for number, total in enumerate(totals):
            row = layer * 8 + number
            value = jnp.sum(total, axis=0, keepdims=True)
            out_ref[row : row + 1] = value + start_ref[row : row + 1] if start_ref is not None else value
    if tables:
        squares_ref, norms_ref, arrived_ref = tables
        out_ref[SQUARES:NORMS] = squares_ref[...]
        out_ref[NORMS:] = norms_ref[...] + arrived_ref[...]


def dots_of(rows, targets, extras=(), offset=0):
    flat = [*rows, *targets.values(), *extras]
    width = [*targets.values()][0].shape[-1]
    return pl.pallas_call(
        functools.partial(dots_kernel, starts=tuple(targets), offset=offset, width=width, extras=len(extras)),
        in_specs=[IN_VMEM] * len(flat),
        out_specs=IN_VMEM,
        out_shape=jax.ShapeDtypeStruct((NORMS + 2 if len(extras) > 1 else SQUARES, LANES), F32),
        compiler_params=pltpu.CompilerParams(vmem_limit_bytes=SMALL_VMEM),
        cost_estimate=pl.CostEstimate(flops=1 << 22, bytes_accessed=3 << 20, transcendentals=0),
        name="dots",
    )(*flat)


def directions_kernel(mine_ref, pair_ref, *refs, count, offset, width):
    block_refs = refs[-4:]
    weights = []
    for layer in range(2):
        mine, pair = mine_ref[8 * layer : 8 * layer + 8], pair_ref[8 * layer : 8 * layer + 8]
        products = jnp.sum(mine + jnp.concatenate([pair[4:], pair[:4]], axis=0), axis=1, keepdims=True)
        row = NORMS + layer
        norm = mine_ref[row : row + 1] + pair_ref[row : row + 1]
        damping = 0.1 * jnp.sum(norm, axis=1, keepdims=True) / count + 1e-06
        squares = []
        for number in range(4):
            row = SQUARES + 2 * layer + number % 2
            squares += [(mine_ref if number < 2 else pair_ref)[row : row + 1]] * 2
        scale = damping + jnp.sum(jnp.concatenate(squares, axis=0), axis=1, keepdims=True)
        weights.append(products / scale)

    def body(at, carry):
        parts = []
        for layer in range(2):
            gradients = []
            for number in range(4):
                ref, place = example_of(refs, layer, number)
                gradients.append(ref[place, :, pl.ds(offset + at, COLUMNS)])
            for target in range(2):
                terms = [weights[layer][2 * n + target : 2 * n + target + 1] * gradients[n] for n in range(4)]
                parts.append(sum(terms[1:], terms[0]))
        for block, ref in enumerate(block_refs):
            pieces = [part[2 * block : 2 * block + 2] for part in parts]
            ref[:, pl.ds(at, COLUMNS)] = jnp.concatenate(pieces, axis=0).astype(ref.dtype)
        return carry

    chunks(width, body, 0)


def directions_of(mine, pair, rows, count, offset, width):
    return pl.pallas_call(
        functools.partial(directions_kernel, count=count, offset=offset, width=width),
        in_specs=[IN_VMEM] * 4,
        out_specs=[IN_VMEM] * 4,
        out_shape=[jax.ShapeDtypeStruct((8, width), kind) for kind in (F32, BF16, BF16, BF16)],
        compiler_params=pltpu.CompilerParams(vmem_limit_bytes=SMALL_VMEM),
        cost_estimate=pl.CostEstimate(flops=1 << 22, bytes_accessed=3 << 20, transcendentals=0),
        name="directions",
    )(mine, pair, *rows)


def turn_kernel(keep_ref, *refs):
    rest_ref, send_ref = refs[-2:]
    total = keep_ref[...]
    for ref in refs[:-2]:
        total += ref[...].astype(F32)
    rest_ref[...] = total
    even = lax.broadcasted_iota(jnp.int32, total.shape, 0) % 2 == 0
    below, above = (jnp.concatenate([total[at:], total[:at]], axis=0) for at in (1, 7))
    send_ref[...] = jnp.where(even, below, above).astype(BF16)


def turned(keep, arrived):
    return pl.pallas_call(
        turn_kernel,
        out_shape=[jax.ShapeDtypeStruct(keep.shape, F32), jax.ShapeDtypeStruct(keep.shape, BF16)],
        compiler_params=pltpu.CompilerParams(vmem_limit_bytes=SMALL_VMEM),
        cost_estimate=pl.CostEstimate(flops=1 << 18, bytes_accessed=1 << 20, transcendentals=0),
        name="add",
    )(keep, *arrived)


def paired_local(inputs, grad_key, grad_value, key_down, key_up, value_down, value_up, validation, lengths):
    layers, examples = inputs.shape[:2]
    count = lax.axis_size("ex") * examples
    index = lax.axis_index("ex").astype(jnp.int32)[None]
    arguments = (index, lengths, inputs, grad_key, grad_value, key_down, key_up, value_down, value_up)

    targets = {0: validation}
    first_bits = (Y | Z1, Z2, Y, Z1)
    for bits in first_bits:
        targets[bits] = swap(validation, bits)
    own, other, squares = gradients_of(*arguments, after=[targets[bits] for bits in first_bits])
    rows = (own, swap(other, CORE))
    for bits in (Y, Z1):
        targets[bits | Z2] = swap(targets[Z2], bits)
    targets[Y | Z1 | Z2] = swap(targets[Z1 | Z2], Y)

    norms = jnp.stack([squares[0] + squares[1], squares[2] + squares[3]])
    for bit in (Y, Z1):
        norms = norms + swap(norms, bit)
    arrived = swap(norms, Z2)

    early = {at: targets[bits] for at, bits in enumerate(SLOTS) if bits in (0, *first_bits)}
    late = {at: targets[bits] for at, bits in enumerate(SLOTS) if bits not in (0, *first_bits)}
    mine = dots_of(rows, late, [dots_of(rows, early), squares, norms, arrived])
    pair = swap(mine, CORE)
    corrections, offset = [], 0
    for width in STREAMS:
        keep, *sends = directions_of(mine, pair, rows, count, offset, width)
        keep, send = turned(keep, [swap(send, bits) for send, bits in zip(sends, QUAD)])
        block = (keep + swap(send, Z2).astype(F32)).astype(BF16)
        blocks = {2 * at: swap(block, bits) if bits else block for at, bits in enumerate((0, *QUAD))}
        corrections = [dots_of(rows, blocks, corrections, offset)]
        offset += width
    damping = 0.1 * jnp.sum(mine[NORMS:] + pair[NORMS:], axis=1) / count + 1e-06
    inner = (mine[:SQUARES] - corrections[0] / count).reshape(layers, 4 * examples, LANES)
    split = 2 * examples
    inner = inner[:, :split] + swap(inner[:, split:], CORE)
    scores = -jnp.sum(jnp.sum(inner, axis=2) / damping[:, None], axis=0)
    return scores.reshape(examples, 2)


def solution(mesh):
    in_specs = (
        P(None, ("groups", "ex"), None, None),
        P(None, ("groups", "ex"), None, None),
        P(None, ("groups", "ex"), None, None),
        P(),
        P(),
        P(),
        P(),
        P(None, "groups", "ex"),
        P(("groups", "ex")),
    )
    out_specs = P(("groups", "ex"), None)

    def local(*arguments):
        low_rank = arguments[3].shape[1]
        row_width = 2 * (arguments[0].shape[3] + arguments[1].shape[3])
        paired = lax.axis_size("ex") == low_rank == 16 and arguments[0].shape[:2] == (2, 2)
        paired = paired and row_width == sum(STREAMS)
        return (paired_local if paired else general_local)(*arguments)

    return jax.shard_map(local, mesh=mesh, in_specs=in_specs, out_specs=out_specs, check_vma=False)
```

```python
import functools

import jax
import jax.numpy as jnp
from jax import lax
from jax.experimental import pallas as pl
from jax.experimental.pallas import tpu as pltpu
from jax.sharding import PartitionSpec as P

F32 = jnp.float32
BF16 = jnp.bfloat16
NN = (((1,), (0,)), ((), ()))
NT = (((1,), (1,)), ((), ()))
LANES = 128
GRADIENT_VMEM = 18 * 1024 * 1024
SMALL_VMEM = 6 * 1024 * 1024


def general_local(inputs, grad_key, grad_value, key_down, key_up, value_down, value_up, validation, lengths):
    highest = lax.Precision.HIGHEST
    num_layers, local_examples, seq_slots, _ = inputs.shape
    total_count = lax.axis_size("ex") * local_examples
    low_rank = key_down.shape[1]
    token_mask = (
        lax.broadcasted_iota(jnp.int32, (local_examples, seq_slots), 1) < lengths[:, None]
    ).astype(F32)
    dot = functools.partial(jnp.einsum, preferred_element_type=F32)

    def masked(values):
        return (values * token_mask[None, :, :, None]).astype(BF16)

    z_key = masked(dot("lesd,lrd->lesr", inputs, key_down))
    z_value = masked(dot("lesd,lrd->lesr", inputs, value_down))
    y_key = masked(dot("leso,lor->lesr", grad_key, key_up))
    y_value = masked(dot("leso,lor->lesr", grad_value, value_up))
    pieces = [
        dot("lesr,lesd->lerd", y_key, inputs),
        dot("lesr,leso->lero", z_key, grad_key),
        dot("lesr,lesd->lerd", y_value, inputs),
        dot("lesr,leso->lero", z_value, grad_value),
    ]
    gradients = jnp.concatenate(pieces, axis=3).reshape(num_layers, local_examples, -1)
    squares = jnp.sum(gradients * gradients, axis=2)
    damping = 0.1 * lax.psum(jnp.sum(squares, axis=1), "ex") / total_count + 1e-06
    targets = lax.all_gather(validation, "ex", axis=2, tiled=True).astype(F32)
    products = jnp.einsum("lep,lvp->lev", gradients, targets, precision=highest)
    weights = products / (damping[:, None, None] + squares[:, :, None])
    directions = jnp.einsum("lev,lep->lvp", weights, gradients, precision=highest)
    summed = lax.psum(directions, "ex")
    correction = jnp.einsum("lep,lvp->lev", gradients, summed, precision=highest)
    inner = products - correction / total_count
    return -jnp.sum(inner / damping[:, None, None], axis=0)


CORE, Y, Z1, Z2 = 1, 2, 4, 8
QUAD = (Z1, Y, Y | Z1)
SLOTS = [bits | last for bits in (0, *QUAD) for last in (0, Z2)]


def swap(values, bit):
    size = lax.axis_size("ex")
    return lax.ppermute(values, "ex", [(index, index ^ bit) for index in range(size)])


def fold_lanes(values):
    tiles = [values[:, at : at + LANES] for at in range(0, values.shape[1], LANES)]
    while len(tiles) > 1:
        tiles = [sum(tiles[at : at + 2]) for at in range(0, len(tiles), 2)]
    return tiles[0]


def rank_order(index, rank):
    half = rank // 2
    row = lax.broadcasted_iota(jnp.int32, (2 * rank, 2 * rank), 0)
    column = lax.broadcasted_iota(jnp.int32, (2 * rank, 2 * rank), 1)
    position = row % half
    relative = position // 4 * Y + position // 2 % 2 * Z1 + position % 2 * Z2 + row // half % 2
    wanted = jnp.bitwise_xor(relative, jnp.broadcast_to(index, relative.shape)) + row // rank * rank
    return (column == wanted).astype(F32).astype(BF16)


def ordered(order, key, value):
    both = jnp.concatenate([key, value], axis=0)
    return lax.dot_general(order, both, NN, preferred_element_type=F32).astype(BF16)


class Unit:
    def __init__(self, number, length, up_factor, gk, gv, outputs):
        self.number, self.gk, self.gv = number, gk, gv
        self.own_ref, self.other_ref, self.square_ref = outputs
        self.seq, self.narrow = gk.shape
        self.rank = up_factor.shape[0] // 2
        token = lax.broadcasted_iota(jnp.int32, (1, self.seq), 1)
        self.mask = (token < length).astype(F32)
        y_key = lax.dot_general(up_factor[: self.rank], gk, NT, preferred_element_type=F32)
        y_value = lax.dot_general(up_factor[self.rank :], gv, NT, preferred_element_type=F32)
        self.y = (jnp.concatenate([y_key, y_value], axis=0) * self.mask).astype(BF16)
        self.z = jnp.zeros((2 * self.rank, self.seq), F32)
        self.total = jnp.zeros((self.rank // 2, LANES), F32)

    def store(self, values, at):
        columns, half = values.shape[1], self.rank // 2
        self.own_ref[self.number, :, at : at + columns] = values[:half]
        self.other_ref[self.number, :, at : at + columns] = values[half:]
        squared = values * values
        self.total += fold_lanes(squared[:half] + squared[half:])

    def chunk(self, factor, x, at, width):
        self.z += lax.dot_general(factor, x, NT, preferred_element_type=F32)
        down = lax.dot_general(self.y, x, NN, preferred_element_type=F32)
        self.store(down[: self.rank], at)
        self.store(down[self.rank :], width + self.narrow + at)

    def finish(self, width):
        z = (self.z * self.mask).astype(BF16)
        self.store(lax.dot_general(z[: self.rank], self.gk, NN, preferred_element_type=F32), width)
        up_value = lax.dot_general(z[self.rank :], self.gv, NN, preferred_element_type=F32)
        self.store(up_value, 2 * width + self.narrow)
        self.square_ref[self.number : self.number + 1] = jnp.sum(self.total, axis=0, keepdims=True)


def gradients_kernel(
    index_ref,
    lengths_ref,
    x_hbm,
    gk_hbm,
    gv_hbm,
    ak_hbm,
    av_hbm,
    bk_hbm,
    bv_hbm,
    own_ref,
    other_ref,
    square_ref,
    x_ref,
    gk_ref,
    gv_ref,
    a_ref,
    b_ref,
    semaphores,
    *,
    chunks,
):
    outputs = (own_ref, other_ref, square_ref)
    layers, _, rank, width = a_ref.shape
    examples = x_ref.shape[1]
    copies = {}

    def start(name, source, target):
        copies[name] = pltpu.make_async_copy(source, target, semaphores.at[len(copies)])
        copies[name].start()

    def wait(*names):
        for name in names:
            copies[name].wait()

    for layer in range(layers):
        start(("bk", layer), bk_hbm.at[layer], b_ref.at[layer, 0])
        start(("bv", layer), bv_hbm.at[layer], b_ref.at[layer, 1])
        start(("gk", layer), gk_hbm.at[layer], gk_ref.at[layer])
        start(("gv", layer), gv_hbm.at[layer], gv_ref.at[layer])
        start(("ak", layer), ak_hbm.at[layer], a_ref.at[layer, 0])
        start(("av", layer), av_hbm.at[layer], a_ref.at[layer, 1])
        for at in range(0, width, chunks[layer]):
            columns = pl.ds(at, chunks[layer])
            start(("x", layer, at), x_hbm.at[layer, :, :, columns], x_ref.at[layer, :, :, columns])

    order = rank_order(index_ref[0], rank)
    for layer in range(layers):
        wait(("bk", layer), ("bv", layer), ("gk", layer), ("gv", layer))
        up_factor = ordered(order, b_ref[layer, 0], b_ref[layer, 1])
        units = [
            Unit(layer * examples + at, lengths_ref[at], up_factor, gk_ref[layer, at], gv_ref[layer, at], outputs)
            for at in range(examples)
        ]
        wait(("ak", layer), ("av", layer))
        for at in range(0, width, COLUMNS * 2):
            columns = slice(at, at + COLUMNS * 2)
            factor = ordered(order, a_ref[layer, 0, :, columns], a_ref[layer, 1, :, columns])
            if at % chunks[layer] == 0:
                wait(("x", layer, at))
            for example, unit in enumerate(units):
                unit.chunk(factor, x_ref[layer, example, :, columns], at, width)
        for unit in units:
            unit.finish(width)


def gate_kernel(*refs):
    pass


IN_VMEM = pl.BlockSpec(memory_space=pltpu.VMEM)
IN_SMEM = pl.BlockSpec(memory_space=pltpu.SMEM)
ANYWHERE = pl.BlockSpec(memory_space=pl.ANY)
COLUMNS = 1024
STREAMS = (9216, 9216)
SQUARES, NORMS = 16, 20


def in_hbm(array):
    return pltpu.with_memory_space_constraint(array, pltpu.HBM)


def gradients_of(index, lengths, inputs, grad_key, grad_value, key_down, key_up, value_down, value_up, after):
    _, _, seq, width = inputs.shape
    narrow = grad_key.shape[3]
    rank = key_down.shape[1]
    rows = jax.ShapeDtypeStruct((4, rank // 2, 2 * (width + narrow)), F32)
    outputs = [rows, rows, jax.ShapeDtypeStruct((4, LANES), F32)]
    lengths = in_hbm(lengths)
    parameters = pltpu.CompilerParams(vmem_limit_bytes=GRADIENT_VMEM)
    own, other, squares = pl.pallas_call(
        functools.partial(gradients_kernel, chunks=(2048, 8192)),
        in_specs=[IN_SMEM] * 2 + [ANYWHERE] * 7,
        out_specs=[IN_VMEM] * 3,
        out_shape=outputs,
        scratch_shapes=[
            pltpu.VMEM((2, 2, seq, width), BF16),
            pltpu.VMEM((2, 2, seq, narrow), BF16),
            pltpu.VMEM((2, 2, seq, narrow), BF16),
            pltpu.VMEM((2, 2, rank, width), BF16),
            pltpu.VMEM((2, 2, rank, narrow), BF16),
            pltpu.SemaphoreType.DMA((17,)),
        ],
        compiler_params=parameters,
        cost_estimate=pl.CostEstimate(flops=1 << 32, bytes_accessed=1 << 24, transcendentals=0),
        name="gradients",
    )(
        index,
        lengths,
        in_hbm(inputs),
        in_hbm(grad_key),
        in_hbm(grad_value),
        in_hbm(key_down),
        in_hbm(value_down),
        in_hbm(jnp.swapaxes(key_up, 1, 2)),
        in_hbm(jnp.swapaxes(value_up, 1, 2)),
    )
    other, squares = pl.pallas_call(
        gate_kernel,
        in_specs=[ANYWHERE] * (2 + len(after)),
        out_specs=[ANYWHERE] * 2,
        out_shape=outputs[1:],
        input_output_aliases={0: 0, 1: 1},
        compiler_params=pltpu.CompilerParams(vmem_limit_bytes=SMALL_VMEM),
        cost_estimate=pl.CostEstimate(flops=1 << 10, bytes_accessed=1 << 10, transcendentals=0),
        name="gate",
    )(other, squares, *after)
    return own, other, squares


def example_of(refs, layer, number):
    return refs[number // 2], 2 * layer + number % 2


def chunks(width, body, init):
    def step(number, carry):
        return body(pl.multiple_of(number * COLUMNS, COLUMNS), carry)

    return lax.fori_loop(0, width // COLUMNS, step, init)


def dots_kernel(*refs, starts, offset, width, extras):
    target_refs = refs[2 : 2 + len(starts)]
    out_ref, extra_refs = refs[-1], refs[-1 - extras : -1]
    start_ref, tables = (extra_refs[0], extra_refs[1:]) if extras else (None, ())
    slots = refs[0].shape[1]
    for layer in range(2):

        def body(at, totals):
            pieces, filled = ([], []), 0
            for start, ref in zip(starts, target_refs):
                columns = pl.ds(at, COLUMNS)
                if len(ref.shape) == 3:
                    values = ref[layer, :, columns].astype(F32)
                else:
                    values = ref[4 * layer : 4 * layer + 4, columns].astype(F32)
                count = values.shape[0] // 2
                for target in range(2):
                    if start > filled:
                        pieces[target].append(jnp.zeros((start - filled, COLUMNS), F32))
                    pieces[target].append(values[target * count : (target + 1) * count])
                filled = start + count
            if filled < slots:
                for target in range(2):
                    pieces[target].append(jnp.zeros((slots - filled, COLUMNS), F32))
            rows = [jnp.concatenate(group, axis=0) for group in pieces]
            updated = []
            for number, total in enumerate(totals):
                ref, place = example_of(refs, layer, number // 2)
                gradient = ref[place, :, pl.ds(offset + at, COLUMNS)]
                updated.append(total + fold_lanes(gradient * rows[number % 2]))
            return tuple(updated)

        totals = chunks(width, body, (jnp.zeros((slots, LANES), F32),) * 8)
        for number, total in enumerate(totals):
            row = layer * 8 + number
            value = jnp.sum(total, axis=0, keepdims=True)
            out_ref[row : row + 1] = value + start_ref[row : row + 1] if start_ref is not None else value
    if tables:
        squares_ref, norms_ref, arrived_ref = tables
        out_ref[SQUARES:NORMS] = squares_ref[...]
        out_ref[NORMS:] = norms_ref[...] + arrived_ref[...]


def dots_of(rows, targets, extras=(), offset=0):
    flat = [*rows, *targets.values(), *extras]
    width = [*targets.values()][0].shape[-1]
    return pl.pallas_call(
        functools.partial(dots_kernel, starts=tuple(targets), offset=offset, width=width, extras=len(extras)),
        in_specs=[IN_VMEM] * len(flat),
        out_specs=IN_VMEM,
        out_shape=jax.ShapeDtypeStruct((NORMS + 2 if len(extras) > 1 else SQUARES, LANES), F32),
        compiler_params=pltpu.CompilerParams(vmem_limit_bytes=SMALL_VMEM),
        cost_estimate=pl.CostEstimate(flops=1 << 22, bytes_accessed=3 << 20, transcendentals=0),
        name="dots",
    )(*flat)


def directions_kernel(mine_ref, pair_ref, *refs, count, offset, width):
    block_refs = refs[-4:]
    weights = []
    for layer in range(2):
        mine, pair = mine_ref[8 * layer : 8 * layer + 8], pair_ref[8 * layer : 8 * layer + 8]
        products = jnp.sum(mine + jnp.concatenate([pair[4:], pair[:4]], axis=0), axis=1, keepdims=True)
        row = NORMS + layer
        norm = mine_ref[row : row + 1] + pair_ref[row : row + 1]
        damping = 0.1 * jnp.sum(norm, axis=1, keepdims=True) / count + 1e-06
        squares = []
        for number in range(4):
            row = SQUARES + 2 * layer + number % 2
            squares += [(mine_ref if number < 2 else pair_ref)[row : row + 1]] * 2
        scale = damping + jnp.sum(jnp.concatenate(squares, axis=0), axis=1, keepdims=True)
        weights.append(products / scale)

    def body(at, carry):
        parts = []
        for layer in range(2):
            gradients = []
            for number in range(4):
                ref, place = example_of(refs, layer, number)
                gradients.append(ref[place, :, pl.ds(offset + at, COLUMNS)])
            for target in range(2):
                terms = [weights[layer][2 * n + target : 2 * n + target + 1] * gradients[n] for n in range(4)]
                parts.append(sum(terms[1:], terms[0]))
        for block, ref in enumerate(block_refs):
            pieces = [part[2 * block : 2 * block + 2] for part in parts]
            ref[:, pl.ds(at, COLUMNS)] = jnp.concatenate(pieces, axis=0).astype(ref.dtype)
        return carry

    chunks(width, body, 0)


def directions_of(mine, pair, rows, count, offset, width):
    return pl.pallas_call(
        functools.partial(directions_kernel, count=count, offset=offset, width=width),
        in_specs=[IN_VMEM] * 4,
        out_specs=[IN_VMEM] * 4,
        out_shape=[jax.ShapeDtypeStruct((8, width), kind) for kind in (F32, BF16, BF16, BF16)],
        compiler_params=pltpu.CompilerParams(vmem_limit_bytes=SMALL_VMEM),
        cost_estimate=pl.CostEstimate(flops=1 << 22, bytes_accessed=3 << 20, transcendentals=0),
        name="directions",
    )(mine, pair, *rows)


def turn_kernel(keep_ref, *refs):
    rest_ref, send_ref = refs[-2:]
    total = keep_ref[...]
    for ref in refs[:-2]:
        total += ref[...].astype(F32)
    rest_ref[...] = total
    even = lax.broadcasted_iota(jnp.int32, total.shape, 0) % 2 == 0
    below, above = (jnp.concatenate([total[at:], total[:at]], axis=0) for at in (1, 7))
    send_ref[...] = jnp.where(even, below, above).astype(BF16)


def turned(keep, arrived):
    return pl.pallas_call(
        turn_kernel,
        out_shape=[jax.ShapeDtypeStruct(keep.shape, F32), jax.ShapeDtypeStruct(keep.shape, BF16)],
        compiler_params=pltpu.CompilerParams(vmem_limit_bytes=SMALL_VMEM),
        cost_estimate=pl.CostEstimate(flops=1 << 18, bytes_accessed=1 << 20, transcendentals=0),
        name="add",
    )(keep, *arrived)


def paired_local(inputs, grad_key, grad_value, key_down, key_up, value_down, value_up, validation, lengths):
    layers, examples = inputs.shape[:2]
    count = lax.axis_size("ex") * examples
    index = lax.axis_index("ex").astype(jnp.int32)[None]
    arguments = (index, lengths, inputs, grad_key, grad_value, key_down, key_up, value_down, value_up)

    targets = {0: validation}
    first_bits = (Y | Z1, Z2, Y, Z1)
    for bits in first_bits:
        targets[bits] = swap(validation, bits)
    own, other, squares = gradients_of(*arguments, after=[targets[bits] for bits in first_bits])
    rows = (own, swap(other, CORE))
    for bits in (Y, Z1):
        targets[bits | Z2] = swap(targets[Z2], bits)
    targets[Y | Z1 | Z2] = swap(targets[Z1 | Z2], Y)

    norms = jnp.stack([squares[0] + squares[1], squares[2] + squares[3]])
    for bit in (Y, Z1):
        norms = norms + swap(norms, bit)
    arrived = swap(norms, Z2)

    early = {at: targets[bits] for at, bits in enumerate(SLOTS) if bits != Y | Z1 | Z2}
    late = {at: targets[bits] for at, bits in enumerate(SLOTS) if bits == Y | Z1 | Z2}
    mine = dots_of(rows, late, [dots_of(rows, early), squares, norms, arrived])
    pair = swap(mine, CORE)
    corrections, offset = [], 0
    for width in STREAMS:
        keep, *sends = directions_of(mine, pair, rows, count, offset, width)
        keep, send = turned(keep, [swap(send, bits) for send, bits in zip(sends, QUAD)])
        block = (keep + swap(send, Z2).astype(F32)).astype(BF16)
        blocks = {0: block, 2: swap(block, Z1), 4: swap(block, Y)}
        is_last = offset + width == sum(STREAMS)
        blocks[6] = swap(block, Y | Z1) if is_last else swap(blocks[2], Y)
        if is_last:
            corrections = [dots_of(rows, {at: blocks.pop(at) for at in (0, 2)}, corrections, offset)]
        corrections = [dots_of(rows, blocks, corrections, offset)]
        offset += width
    damping = 0.1 * jnp.sum(mine[NORMS:] + pair[NORMS:], axis=1) / count + 1e-06
    inner = (mine[:SQUARES] - corrections[0] / count).reshape(layers, 4 * examples, LANES)
    split = 2 * examples
    inner = inner[:, :split] + swap(inner[:, split:], CORE)
    scores = -jnp.sum(jnp.sum(inner, axis=2) / damping[:, None], axis=0)
    return scores.reshape(examples, 2)


def solution(mesh):
    in_specs = (
        P(None, ("groups", "ex"), None, None),
        P(None, ("groups", "ex"), None, None),
        P(None, ("groups", "ex"), None, None),
        P(),
        P(),
        P(),
        P(),
        P(None, "groups", "ex"),
        P(("groups", "ex")),
    )
    out_specs = P(("groups", "ex"), None)

    def local(*arguments):
        low_rank = arguments[3].shape[1]
        row_width = 2 * (arguments[0].shape[3] + arguments[1].shape[3])
        paired = lax.axis_size("ex") == low_rank == 16 and arguments[0].shape[:2] == (2, 2)
        paired = paired and row_width == sum(STREAMS)
        return (paired_local if paired else general_local)(*arguments)

    return jax.shard_map(local, mesh=mesh, in_specs=in_specs, out_specs=out_specs, check_vma=False)
```

```python
import functools

import jax
import jax.numpy as jnp
from jax import lax
from jax.experimental import pallas as pl
from jax.experimental.pallas import tpu as pltpu
from jax.sharding import PartitionSpec as P

F32 = jnp.float32
BF16 = jnp.bfloat16
NN = (((1,), (0,)), ((), ()))
NT = (((1,), (1,)), ((), ()))
LANES = 128
GRADIENT_VMEM = 18 * 1024 * 1024
SMALL_VMEM = 6 * 1024 * 1024


def general_local(inputs, grad_key, grad_value, key_down, key_up, value_down, value_up, validation, lengths):
    highest = lax.Precision.HIGHEST
    num_layers, local_examples, seq_slots, _ = inputs.shape
    total_count = lax.axis_size("ex") * local_examples
    low_rank = key_down.shape[1]
    token_mask = (
        lax.broadcasted_iota(jnp.int32, (local_examples, seq_slots), 1) < lengths[:, None]
    ).astype(F32)
    dot = functools.partial(jnp.einsum, preferred_element_type=F32)

    def masked(values):
        return (values * token_mask[None, :, :, None]).astype(BF16)

    z_key = masked(dot("lesd,lrd->lesr", inputs, key_down))
    z_value = masked(dot("lesd,lrd->lesr", inputs, value_down))
    y_key = masked(dot("leso,lor->lesr", grad_key, key_up))
    y_value = masked(dot("leso,lor->lesr", grad_value, value_up))
    pieces = [
        dot("lesr,lesd->lerd", y_key, inputs),
        dot("lesr,leso->lero", z_key, grad_key),
        dot("lesr,lesd->lerd", y_value, inputs),
        dot("lesr,leso->lero", z_value, grad_value),
    ]
    gradients = jnp.concatenate(pieces, axis=3).reshape(num_layers, local_examples, -1)
    squares = jnp.sum(gradients * gradients, axis=2)
    damping = 0.1 * lax.psum(jnp.sum(squares, axis=1), "ex") / total_count + 1e-06
    targets = lax.all_gather(validation, "ex", axis=2, tiled=True).astype(F32)
    products = jnp.einsum("lep,lvp->lev", gradients, targets, precision=highest)
    weights = products / (damping[:, None, None] + squares[:, :, None])
    directions = jnp.einsum("lev,lep->lvp", weights, gradients, precision=highest)
    summed = lax.psum(directions, "ex")
    correction = jnp.einsum("lep,lvp->lev", gradients, summed, precision=highest)
    inner = products - correction / total_count
    return -jnp.sum(inner / damping[:, None, None], axis=0)


CORE, Y, Z1, Z2 = 1, 2, 4, 8
QUAD = (Z1, Y, Y | Z1)
SLOTS = [bits | last for bits in (0, *QUAD) for last in (0, Z2)]


def swap(values, bit):
    size = lax.axis_size("ex")
    return lax.ppermute(values, "ex", [(index, index ^ bit) for index in range(size)])


def fold_lanes(values):
    tiles = [values[:, at : at + LANES] for at in range(0, values.shape[1], LANES)]
    while len(tiles) > 1:
        tiles = [sum(tiles[at : at + 2]) for at in range(0, len(tiles), 2)]
    return tiles[0]


def rank_order(index, rank):
    half = rank // 2
    row = lax.broadcasted_iota(jnp.int32, (2 * rank, 2 * rank), 0)
    column = lax.broadcasted_iota(jnp.int32, (2 * rank, 2 * rank), 1)
    position = row % half
    relative = position // 4 * Y + position // 2 % 2 * Z1 + position % 2 * Z2 + row // half % 2
    wanted = jnp.bitwise_xor(relative, jnp.broadcast_to(index, relative.shape)) + row // rank * rank
    return (column == wanted).astype(F32).astype(BF16)


def ordered(order, key, value):
    both = jnp.concatenate([key, value], axis=0)
    return lax.dot_general(order, both, NN, preferred_element_type=F32).astype(BF16)


class Unit:
    def __init__(self, number, length, up_factor, gk, gv, outputs):
        self.number, self.gk, self.gv = number, gk, gv
        self.own_ref, self.other_ref, self.square_ref = outputs
        self.seq, self.narrow = gk.shape
        self.rank = up_factor.shape[0] // 2
        token = lax.broadcasted_iota(jnp.int32, (1, self.seq), 1)
        self.mask = (token < length).astype(F32)
        y_key = lax.dot_general(up_factor[: self.rank], gk, NT, preferred_element_type=F32)
        y_value = lax.dot_general(up_factor[self.rank :], gv, NT, preferred_element_type=F32)
        self.y = (jnp.concatenate([y_key, y_value], axis=0) * self.mask).astype(BF16)
        self.z = jnp.zeros((2 * self.rank, self.seq), F32)
        self.total = jnp.zeros((self.rank // 2, LANES), F32)

    def store(self, values, at):
        columns, half = values.shape[1], self.rank // 2
        self.own_ref[self.number, :, at : at + columns] = values[:half]
        self.other_ref[self.number, :, at : at + columns] = values[half:]
        squared = values * values
        self.total += fold_lanes(squared[:half] + squared[half:])

    def chunk(self, factor, x, at, width):
        self.z += lax.dot_general(factor, x, NT, preferred_element_type=F32)
        down = lax.dot_general(self.y, x, NN, preferred_element_type=F32)
        self.store(down[: self.rank], at)
        self.store(down[self.rank :], width + self.narrow + at)

    def finish(self, width):
        z = (self.z * self.mask).astype(BF16)
        self.store(lax.dot_general(z[: self.rank], self.gk, NN, preferred_element_type=F32), width)
        up_value = lax.dot_general(z[self.rank :], self.gv, NN, preferred_element_type=F32)
        self.store(up_value, 2 * width + self.narrow)
        self.square_ref[self.number : self.number + 1] = jnp.sum(self.total, axis=0, keepdims=True)


def gradients_kernel(
    index_ref,
    lengths_ref,
    x_hbm,
    gk_hbm,
    gv_hbm,
    ak_hbm,
    av_hbm,
    bk_hbm,
    bv_hbm,
    own_ref,
    other_ref,
    square_ref,
    x_ref,
    gk_ref,
    gv_ref,
    a_ref,
    b_ref,
    semaphores,
    *,
    chunks,
):
    outputs = (own_ref, other_ref, square_ref)
    layers, _, rank, width = a_ref.shape
    examples = x_ref.shape[1]
    copies = {}

    def start(name, source, target):
        copies[name] = pltpu.make_async_copy(source, target, semaphores.at[len(copies)])
        copies[name].start()

    def wait(*names):
        for name in names:
            copies[name].wait()

    for layer in range(layers):
        start(("bk", layer), bk_hbm.at[layer], b_ref.at[layer, 0])
        start(("bv", layer), bv_hbm.at[layer], b_ref.at[layer, 1])
        start(("gk", layer), gk_hbm.at[layer], gk_ref.at[layer])
        start(("gv", layer), gv_hbm.at[layer], gv_ref.at[layer])
        start(("ak", layer), ak_hbm.at[layer], a_ref.at[layer, 0])
        start(("av", layer), av_hbm.at[layer], a_ref.at[layer, 1])
        for at in range(0, width, chunks[layer]):
            columns = pl.ds(at, chunks[layer])
            start(("x", layer, at), x_hbm.at[layer, :, :, columns], x_ref.at[layer, :, :, columns])

    order = rank_order(index_ref[0], rank)
    for layer in range(layers):
        wait(("bk", layer), ("bv", layer), ("gk", layer), ("gv", layer))
        up_factor = ordered(order, b_ref[layer, 0], b_ref[layer, 1])
        units = [
            Unit(layer * examples + at, lengths_ref[at], up_factor, gk_ref[layer, at], gv_ref[layer, at], outputs)
            for at in range(examples)
        ]
        wait(("ak", layer), ("av", layer))
        for at in range(0, width, INPUT_COLUMNS):
            columns = slice(at, at + INPUT_COLUMNS)
            factor = ordered(order, a_ref[layer, 0, :, columns], a_ref[layer, 1, :, columns])
            if at % chunks[layer] == 0:
                wait(("x", layer, at))
            for example, unit in enumerate(units):
                unit.chunk(factor, x_ref[layer, example, :, columns], at, width)
        for unit in units:
            unit.finish(width)


def gate_kernel(*refs):
    pass


IN_VMEM = pl.BlockSpec(memory_space=pltpu.VMEM)
IN_SMEM = pl.BlockSpec(memory_space=pltpu.SMEM)
ANYWHERE = pl.BlockSpec(memory_space=pl.ANY)
COLUMNS = 1536
INPUT_COLUMNS = 2048
STREAMS = (9216, 9216)
SQUARES, NORMS = 16, 20


def in_hbm(array):
    return pltpu.with_memory_space_constraint(array, pltpu.HBM)


def gradients_of(index, lengths, inputs, grad_key, grad_value, key_down, key_up, value_down, value_up, after):
    _, _, seq, width = inputs.shape
    narrow = grad_key.shape[3]
    rank = key_down.shape[1]
    rows = jax.ShapeDtypeStruct((4, rank // 2, 2 * (width + narrow)), F32)
    outputs = [rows, rows, jax.ShapeDtypeStruct((4, LANES), F32)]
    lengths = in_hbm(lengths)
    parameters = pltpu.CompilerParams(vmem_limit_bytes=GRADIENT_VMEM)
    own, other, squares = pl.pallas_call(
        functools.partial(gradients_kernel, chunks=(INPUT_COLUMNS, width)),
        in_specs=[IN_SMEM] * 2 + [ANYWHERE] * 7,
        out_specs=[IN_VMEM] * 3,
        out_shape=outputs,
        scratch_shapes=[
            pltpu.VMEM((2, 2, seq, width), BF16),
            pltpu.VMEM((2, 2, seq, narrow), BF16),
            pltpu.VMEM((2, 2, seq, narrow), BF16),
            pltpu.VMEM((2, 2, rank, width), BF16),
            pltpu.VMEM((2, 2, rank, narrow), BF16),
            pltpu.SemaphoreType.DMA((17,)),
        ],
        compiler_params=parameters,
        cost_estimate=pl.CostEstimate(flops=1 << 32, bytes_accessed=1 << 24, transcendentals=0),
        name="gradients",
    )(
        index,
        lengths,
        in_hbm(inputs),
        in_hbm(grad_key),
        in_hbm(grad_value),
        in_hbm(key_down),
        in_hbm(value_down),
        in_hbm(jnp.swapaxes(key_up, 1, 2)),
        in_hbm(jnp.swapaxes(value_up, 1, 2)),
    )
    other, squares = pl.pallas_call(
        gate_kernel,
        in_specs=[ANYWHERE] * (2 + len(after)),
        out_specs=[ANYWHERE] * 2,
        out_shape=outputs[1:],
        input_output_aliases={0: 0, 1: 1},
        compiler_params=pltpu.CompilerParams(vmem_limit_bytes=SMALL_VMEM),
        cost_estimate=pl.CostEstimate(flops=1 << 10, bytes_accessed=1 << 10, transcendentals=0),
        name="gate",
    )(other, squares, *after)
    return own, other, squares


def example_of(refs, layer, number):
    return refs[number // 2], 2 * layer + number % 2


def chunks(width, body, init):
    def step(number, carry):
        return body(pl.multiple_of(number * COLUMNS, COLUMNS), carry)

    return lax.fori_loop(0, width // COLUMNS, step, init)


def dots_kernel(*refs, starts, offset, width, extras):
    target_refs = refs[2 : 2 + len(starts)]
    out_ref, extra_refs = refs[-1], refs[-1 - extras : -1]
    start_ref, tables = (extra_refs[0], extra_refs[1:]) if extras else (None, ())
    slots = refs[0].shape[1]
    for layer in range(2):

        def body(at, totals):
            pieces, filled = ([], []), 0
            for start, ref in zip(starts, target_refs):
                columns = pl.ds(at, COLUMNS)
                if len(ref.shape) == 3:
                    values = ref[layer, :, columns].astype(F32)
                else:
                    values = ref[4 * layer : 4 * layer + 4, columns].astype(F32)
                count = values.shape[0] // 2
                for target in range(2):
                    if start > filled:
                        pieces[target].append(jnp.zeros((start - filled, COLUMNS), F32))
                    pieces[target].append(values[target * count : (target + 1) * count])
                filled = start + count
            if filled < slots:
                for target in range(2):
                    pieces[target].append(jnp.zeros((slots - filled, COLUMNS), F32))
            rows = [jnp.concatenate(group, axis=0) for group in pieces]
            updated = []
            for number, total in enumerate(totals):
                ref, place = example_of(refs, layer, number // 2)
                gradient = ref[place, :, pl.ds(offset + at, COLUMNS)]
                updated.append(total + fold_lanes(gradient * rows[number % 2]))
            return tuple(updated)

        totals = chunks(width, body, (jnp.zeros((slots, LANES), F32),) * 8)
        for number, total in enumerate(totals):
            row = layer * 8 + number
            value = jnp.sum(total, axis=0, keepdims=True)
            out_ref[row : row + 1] = value + start_ref[row : row + 1] if start_ref is not None else value
    if tables:
        squares_ref, norms_ref, arrived_ref = tables
        out_ref[SQUARES:NORMS] = squares_ref[...]
        out_ref[NORMS:] = norms_ref[...] + arrived_ref[...]


def dots_of(rows, targets, extras=(), offset=0):
    flat = [*rows, *targets.values(), *extras]
    width = [*targets.values()][0].shape[-1]
    return pl.pallas_call(
        functools.partial(dots_kernel, starts=tuple(targets), offset=offset, width=width, extras=len(extras)),
        in_specs=[IN_VMEM] * len(flat),
        out_specs=IN_VMEM,
        out_shape=jax.ShapeDtypeStruct((NORMS + 2 if len(extras) > 1 else SQUARES, LANES), F32),
        compiler_params=pltpu.CompilerParams(vmem_limit_bytes=SMALL_VMEM),
        cost_estimate=pl.CostEstimate(flops=1 << 22, bytes_accessed=3 << 20, transcendentals=0),
        name="dots",
    )(*flat)


def directions_kernel(mine_ref, pair_ref, *refs, count, offset, width):
    block_refs = refs[-4:]
    weights = []
    for layer in range(2):
        mine, pair = mine_ref[8 * layer : 8 * layer + 8], pair_ref[8 * layer : 8 * layer + 8]
        products = jnp.sum(mine + jnp.concatenate([pair[4:], pair[:4]], axis=0), axis=1, keepdims=True)
        row = NORMS + layer
        norm = mine_ref[row : row + 1] + pair_ref[row : row + 1]
        damping = 0.1 * jnp.sum(norm, axis=1, keepdims=True) / count + 1e-06
        squares = []
        for number in range(4):
            row = SQUARES + 2 * layer + number % 2
            squares += [(mine_ref if number < 2 else pair_ref)[row : row + 1]] * 2
        scale = damping + jnp.sum(jnp.concatenate(squares, axis=0), axis=1, keepdims=True)
        weights.append(products / scale)

    def body(at, carry):
        parts = []
        for layer in range(2):
            gradients = []
            for number in range(4):
                ref, place = example_of(refs, layer, number)
                gradients.append(ref[place, :, pl.ds(offset + at, COLUMNS)])
            for target in range(2):
                terms = [weights[layer][2 * n + target : 2 * n + target + 1] * gradients[n] for n in range(4)]
                parts.append(sum(terms[1:], terms[0]))
        for block, ref in enumerate(block_refs):
            pieces = [part[2 * block : 2 * block + 2] for part in parts]
            ref[:, pl.ds(at, COLUMNS)] = jnp.concatenate(pieces, axis=0).astype(ref.dtype)
        return carry

    chunks(width, body, 0)


def directions_of(mine, pair, rows, count, offset, width):
    return pl.pallas_call(
        functools.partial(directions_kernel, count=count, offset=offset, width=width),
        in_specs=[IN_VMEM] * 4,
        out_specs=[IN_VMEM] * 4,
        out_shape=[jax.ShapeDtypeStruct((8, width), kind) for kind in (F32, BF16, BF16, BF16)],
        compiler_params=pltpu.CompilerParams(vmem_limit_bytes=SMALL_VMEM),
        cost_estimate=pl.CostEstimate(flops=1 << 22, bytes_accessed=3 << 20, transcendentals=0),
        name="directions",
    )(mine, pair, *rows)


def turn_kernel(keep_ref, *refs):
    rest_ref, send_ref = refs[-2:]
    total = keep_ref[...]
    for ref in refs[:-2]:
        total += ref[...].astype(F32)
    rest_ref[...] = total
    even = lax.broadcasted_iota(jnp.int32, total.shape, 0) % 2 == 0
    below, above = (jnp.concatenate([total[at:], total[:at]], axis=0) for at in (1, 7))
    send_ref[...] = jnp.where(even, below, above).astype(BF16)


def turned(keep, arrived):
    return pl.pallas_call(
        turn_kernel,
        out_shape=[jax.ShapeDtypeStruct(keep.shape, F32), jax.ShapeDtypeStruct(keep.shape, BF16)],
        compiler_params=pltpu.CompilerParams(vmem_limit_bytes=SMALL_VMEM),
        cost_estimate=pl.CostEstimate(flops=1 << 18, bytes_accessed=1 << 20, transcendentals=0),
        name="add",
    )(keep, *arrived)


def paired_local(inputs, grad_key, grad_value, key_down, key_up, value_down, value_up, validation, lengths):
    layers, examples = inputs.shape[:2]
    count = lax.axis_size("ex") * examples
    index = lax.axis_index("ex").astype(jnp.int32)[None]
    arguments = (index, lengths, inputs, grad_key, grad_value, key_down, key_up, value_down, value_up)

    targets = {0: validation}
    first_bits = (Y | Z1, Z2, Y, Z1)
    for bits in first_bits:
        targets[bits] = swap(validation, bits)
    own, other, squares = gradients_of(*arguments, after=[targets[bits] for bits in first_bits])
    rows = (own, swap(other, CORE))
    for bits in (Y, Z1):
        targets[bits | Z2] = swap(targets[Z2], bits)
    targets[Y | Z1 | Z2] = swap(targets[Z1 | Z2], Y)

    norms = jnp.stack([squares[0] + squares[1], squares[2] + squares[3]])
    for bit in (Y, Z1):
        norms = norms + swap(norms, bit)
    arrived = swap(norms, Z2)

    early = {at: targets[bits] for at, bits in enumerate(SLOTS) if bits != Y | Z1 | Z2}
    late = {at: targets[bits] for at, bits in enumerate(SLOTS) if bits == Y | Z1 | Z2}
    mine = dots_of(rows, late, [dots_of(rows, early), squares, norms, arrived])
    pair = swap(mine, CORE)
    corrections, offset = [], 0
    for width in STREAMS:
        keep, *sends = directions_of(mine, pair, rows, count, offset, width)
        keep, send = turned(keep, [swap(send, bits) for send, bits in zip(sends, QUAD)])
        block = (keep + swap(send, Z2).astype(F32)).astype(BF16)
        blocks = {0: block, 2: swap(block, Z1), 4: swap(block, Y)}
        is_last = offset + width == sum(STREAMS)
        blocks[6] = swap(block, Y | Z1) if is_last else swap(blocks[2], Y)
        if is_last:
            corrections = [dots_of(rows, {at: blocks.pop(at) for at in (0, 2)}, corrections, offset)]
        corrections = [dots_of(rows, blocks, corrections, offset)]
        offset += width
    damping = 0.1 * jnp.sum(mine[NORMS:] + pair[NORMS:], axis=1) / count + 1e-06
    inner = (mine[:SQUARES] - corrections[0] / count).reshape(layers, 4 * examples, LANES)
    split = 2 * examples
    inner = inner[:, :split] + swap(inner[:, split:], CORE)
    scores = -jnp.sum(jnp.sum(inner, axis=2) / damping[:, None], axis=0)
    return scores.reshape(examples, 2)


def solution(mesh):
    in_specs = (
        P(None, ("groups", "ex"), None, None),
        P(None, ("groups", "ex"), None, None),
        P(None, ("groups", "ex"), None, None),
        P(),
        P(),
        P(),
        P(),
        P(None, "groups", "ex"),
        P(("groups", "ex")),
    )
    out_specs = P(("groups", "ex"), None)

    def local(*arguments):
        low_rank = arguments[3].shape[1]
        row_width = 2 * (arguments[0].shape[3] + arguments[1].shape[3])
        paired = lax.axis_size("ex") == low_rank == 16 and arguments[0].shape[:2] == (2, 2)
        paired = paired and row_width == sum(STREAMS)
        return (paired_local if paired else general_local)(*arguments)

    return jax.shard_map(local, mesh=mesh, in_specs=in_specs, out_specs=out_specs, check_vma=False)
```
